128 devices in a mesh: dp: 1, ctx: 16 (over y, x), tp: 8 (over z, core).
Axes of the slice: x: 4, y: 4, z: 4, core: 2. Of those that a mesh axis runs over, the one named last changes fastest.
Arguments:
- tokens: bfloat16 [4096, 4096], P(('dp', 'ctx', 'tp')), may hold values from -400 to 400
- projection: bfloat16 [4096, 6144], P('ctx', 'tp'), may hold values from -0.09375 to 0.09375
- norm_gain: float32 [4096], replicated, may hold values from 0.5 to 1.5
- query_gain: float32 [128], replicated, may hold values from 0.1 to 1.9
- key_gain: float32 [128], replicated, may hold values from 0.1 to 1.9
- segment_ids: int32 [4096], P('dp'), may hold values from 0 to 15, never falling along the last dimension, each value on 1 to 3072 neighbouring positions
- context_cotangent: bfloat16 [4096, 4096], P(('dp', 'ctx'), 'tp'), may hold values from -48 to 48
Outputs:
- context: bfloat16 [4096, 4096], P(('dp', 'ctx'), 'tp')
- token_grads: float32 [4096, 4096], P(('dp', 'ctx', 'tp'))
- projection_grads: float32 [4096, 6144], P(('dp', 'ctx'), 'tp')
- norm_gain_grads: float32 [4096], P('dp')
- query_gain_grads: float32 [128], P('dp')
- key_gain_grads: float32 [128], P('dp')
The draws below stay inside these ranges and needn't reach their ends.
Inputs may be any that keep to these rules, and one draw needn't show every extreme that they name: `segment_ids`: never falls along the document; each sub-document holds 1 to 3072 tokens, and one holds exactly that many.
All inputs are finite; a program needn't handle non-finite values.
Results may differ from the reference program's by a relative error of at most 0.02.
Values may be sent and summed in bfloat16 or wider, within the bound.
A program may use at most 128 MiB of HBM per device.

```python
import math
import jax
import jax.numpy as jnp
import numpy as np
from jax import lax

D = 4096
HQ = 32
KEY_HEADS = 8
HEAD_WIDTH = 128
QUERY_PER_KEY = 4
QKV_COLS = 6144
TOKENS_PER_SHARD = 256
TOKENS = 4096
N_CTX = 16


def draw_tokens(key, part):
    key = jax.random.fold_in(key, 3)
    first, second, third = jax.random.split(key, 3)
    row_scale = jnp.exp(jax.random.uniform(second, (TOKENS, 1), jnp.float32, 0.0, 2.3))
    column_scale = jnp.exp(jax.random.uniform(third, (1, D), jnp.float32, 0.0, 2.3))
    sample = jnp.clip(jax.random.normal(first, (TOKENS, D), jnp.float32), -4.0, 4.0)
    return (sample * row_scale * column_scale).astype(jnp.bfloat16)


def draw_context_cotangent(key, part):
    key = jax.random.fold_in(key, 7)
    first, second = jax.random.split(key, 2)
    rising = 1.0 + 2.0 * jnp.arange(TOKENS, dtype=jnp.float32) / TOKENS
    token_scale = jnp.exp(jax.random.uniform(second, (TOKENS, 1), jnp.float32, 0.0, 2.3))
    sample = jnp.clip(jax.random.normal(first, (TOKENS, HQ * HEAD_WIDTH), jnp.float32), -4.0, 4.0)
    return (sample * token_scale * rising[:, None] * 0.3).astype(jnp.bfloat16)


def block_levels(stream_key, shape, cuts, smallest, high):
    level = 1.0
    for axis_at, parts in cuts:
        heights = jax.random.uniform(jax.random.fold_in(jax.random.fold_in(stream_key, 6), axis_at), (parts,), jnp.float32, smallest / len(cuts), high / len(cuts))
        level = level * jnp.repeat(jnp.exp(heights), shape[axis_at] // parts).reshape((-1,) + (1,) * (len(shape) - 1 - axis_at))
    return level


def length_profile(number_of, total, reach, lean):
    loads = [(1 << 20) // math.isqrt(grade ** lean) + 1 for grade in range(2, number_of + 1)]
    spare, given = total - reach - (number_of - 1), [1] * (number_of - 1)
    while spare > 0:
        free = [i for i in range(number_of - 1) if given[i] < reach]
        whole, left = sum([loads[i] for i in free]), spare
        for i in free:
            more = min(reach - given[i], max(1, left * loads[i] // whole), spare)
            given[i] = given[i] + more
            spare = spare - more
    return np.array([reach] + given)


def ragged_sizes(rng, number_of, total, limit, slope):
    if number_of == 2:
        one = jax.random.randint(rng, (), max(1, total - limit), min(limit, total - 1) + 1)
        return jnp.stack([one, total - one])
    tallies = jnp.asarray(length_profile(number_of, total, limit, slope), jnp.int32)
    pairs = (number_of - 1) // 2
    source_of, taker = tallies[1:1 + 2 * pairs:2], tallies[2:2 + 2 * pairs:2]
    room = jnp.minimum(source_of - 1, limit - taker)
    passed = jax.random.randint(jax.random.fold_in(rng, 1), (pairs,), 0, 1 << 20) % (room + 1)
    tallies = tallies.at[1:1 + 2 * pairs:2].set(source_of - passed).at[2:2 + 2 * pairs:2].set(taker + passed)
    return tallies[jax.random.permutation(jax.random.fold_in(rng, 2), number_of)]


def noise(own_key, extent, scale, reach, pieces=(), kind=jnp.bfloat16):
    drawn = scale * jax.random.normal(own_key, extent, jnp.float32)
    if pieces:
        drawn = drawn * block_levels(own_key, extent, pieces, -0.22, 0.18)
    return jnp.clip(drawn, -reach, reach).astype(kind)


def setup_inputs(seed: int = 0, part: int = 0) -> dict:
    splits = jax.random.split(jax.random.key(seed), 8)
    own_keys = jax.random.split(jax.random.fold_in(splits[7], part), 8)
    return {
        "tokens": draw_tokens(jax.random.fold_in(jax.random.fold_in(splits[7], part), 71), part),
        "projection": noise(splits[1], (D, QKV_COLS), D ** -0.5, 0.09375, ((0, 16), (1, 8))),
        "norm_gain": jnp.clip(1.0 + 0.1 * jax.random.normal(splits[2], (D,), jnp.float32), 0.5, 1.5),
        "query_gain": jnp.clip(1.0 + 0.18 * jax.random.normal(splits[3], (HEAD_WIDTH,), jnp.float32), 0.1, 1.9),
        "key_gain": jnp.clip(1.0 + 0.18 * jax.random.normal(splits[4], (HEAD_WIDTH,), jnp.float32), 0.1, 1.9),
        "segment_ids": jnp.searchsorted(jnp.cumsum(ragged_sizes(own_keys[5], N_CTX, TOKENS, 3 * TOKENS // 4, 2)), jnp.arange(TOKENS), side="right").astype(jnp.int32),
        "context_cotangent": draw_context_cotangent(jax.random.fold_in(jax.random.fold_in(splits[7], part), 71), part),
    }


EPSILON = 1e-06
THETA = 1000000.0

def rms_norm(values, gain):
    mean_square = lax.optimization_barrier(jnp.mean(values * values, axis=-1, keepdims=True))
    return values * lax.rsqrt(mean_square + EPSILON) * gain

def rope_tables(positions, width):
    half = width // 2
    frequency = THETA ** (-2.0 * jnp.arange(half, dtype=jnp.float32) / width)
    angles = positions.astype(jnp.float32)[:, None] * frequency[None, :]
    return (jnp.cos(angles), jnp.sin(angles))

def rotate(values, cosine, sine):
    half = values.shape[-1] // 2
    layout = (cosine.shape[0],) + (1,) * (values.ndim - 2) + (half,)
    cosine = cosine.reshape(layout)
    sine = sine.reshape(layout)
    first = values[..., :half]
    second = values[..., half:]
    return jnp.concatenate([first * cosine - second * sine, second * cosine + first * sine], axis=-1)

def round_trip(values):
    return lax.optimization_barrier(values.astype(jnp.bfloat16)).astype(jnp.float32)

def reference(tokens, projection, norm_gain, query_gain, key_gain, segment_ids, context_cotangent):
    total_sum = tokens.shape[0]
    scale = HEAD_WIDTH ** (-0.5)
    tokens_wide = tokens.astype(jnp.float32)
    normed_values = rms_norm(tokens_wide, norm_gain).astype(jnp.bfloat16)
    joined_rows = jnp.dot(normed_values, projection, preferred_element_type=jnp.float32).reshape(total_sum, KEY_HEADS, QUERY_PER_KEY + 2, HEAD_WIDTH)
    query_raw = joined_rows[:, :, :QUERY_PER_KEY, :]
    key_raw = joined_rows[:, :, QUERY_PER_KEY, :]
    value_raw = joined_rows[:, :, QUERY_PER_KEY + 1, :]
    cosine, sine = rope_tables(jnp.arange(total_sum, dtype=jnp.int32), HEAD_WIDTH)

    def head_map(raw, gain):
        return rotate(rms_norm(raw, gain), cosine, sine)
    queries = head_map(query_raw, query_gain).astype(jnp.bfloat16)
    keys = head_map(key_raw, key_gain).astype(jnp.bfloat16)
    values = value_raw.astype(jnp.bfloat16)
    same_segment = segment_ids[:, None] == segment_ids[None, :]
    upstream_gradient = context_cotangent.reshape(total_sum, KEY_HEADS, QUERY_PER_KEY, HEAD_WIDTH)

    def per_group(operands):
        query_block, key_block, value_block, upstream_block = operands
        query_wide = query_block.astype(jnp.float32)
        key_wide = key_block.astype(jnp.float32)
        value_wide = value_block.astype(jnp.float32)
        upstream_wide = upstream_block.astype(jnp.float32)
        scores = jnp.einsum('tgd,sd->gts', query_wide, key_wide) * scale
        exponent = jnp.where(same_segment[None], jnp.exp(scores), 0.0)
        denominator = lax.optimization_barrier(jnp.sum(exponent, axis=-1))
        numerator = jnp.einsum('gts,sd->tgd', round_trip(exponent), value_wide)
        context_block = (numerator / denominator.T[:, :, None]).astype(jnp.bfloat16)
        probabilities = exponent / denominator[:, :, None]
        prob_grads = jnp.einsum('tgd,sd->gts', upstream_wide, value_wide)
        correction = lax.optimization_barrier(jnp.sum(upstream_wide * context_block.astype(jnp.float32), axis=-1)).T
        score_grads = round_trip(probabilities * (prob_grads - correction[:, :, None]))
        query_grads = jnp.einsum('gts,sd->tgd', score_grads, key_wide) * scale
        key_grads = jnp.einsum('gts,tgd->sd', score_grads, query_wide) * scale
        value_gradient = jnp.einsum('gts,tgd->sd', round_trip(probabilities), upstream_wide)
        return (context_block, query_grads, key_grads, value_gradient)
    context_heads, query_grads, key_grads, value_gradient = lax.map(per_group, (jnp.transpose(queries, (1, 0, 2, 3)), jnp.transpose(keys, (1, 0, 2)), jnp.transpose(values, (1, 0, 2)), jnp.transpose(upstream_gradient, (1, 0, 2, 3))))
    context = jnp.transpose(context_heads, (1, 0, 2, 3)).reshape(total_sum, HQ * HEAD_WIDTH)
    query_grads = jnp.transpose(query_grads, (1, 0, 2, 3))
    key_grads = jnp.transpose(key_grads, (1, 0, 2))
    value_gradient = jnp.transpose(value_gradient, (1, 0, 2))
    mapped, query_back = jax.vjp(head_map, query_raw, query_gain)
    unnormed_query_gradient, query_gain_grads = query_back(query_grads)
    mapped, key_back = jax.vjp(head_map, key_raw, key_gain)
    unnormed_key_gradient, key_gain_grads = key_back(key_grads)
    joined_gradient = jnp.concatenate([unnormed_query_gradient, unnormed_key_gradient[:, :, None, :], value_gradient[:, :, None, :]], axis=2).reshape(total_sum, KEY_HEADS * (QUERY_PER_KEY + 2) * HEAD_WIDTH).astype(jnp.bfloat16)
    normed_blocks = normed_values.reshape(N_CTX, TOKENS_PER_SHARD, D)
    gradient_blocks = joined_gradient.reshape(N_CTX, TOKENS_PER_SHARD, KEY_HEADS * (QUERY_PER_KEY + 2) * HEAD_WIDTH)

    def add_block(running, pair):
        term = lax.dot_general(pair[0], pair[1], (((0,), (0,)), ((), ())), preferred_element_type=jnp.float32)
        return (running + round_trip(term), None)
    projection_grads, unused = lax.scan(add_block, jnp.zeros(projection.shape, jnp.float32), (normed_blocks, gradient_blocks))
    normed_grads = lax.dot_general(joined_gradient, projection, (((1,), (1,)), ((), ())), preferred_element_type=jnp.float32)
    mapped, norm_back = jax.vjp(rms_norm, tokens_wide, norm_gain)
    token_grads, norm_gain_grads = norm_back(normed_grads)
    return (context, token_grads, projection_grads, norm_gain_grads, query_gain_grads, key_gain_grads)
```

```python
import jax
import jax.numpy as jnp
from jax import lax
from jax.experimental import pallas as pl
from jax.experimental.pallas import tpu as pltpu
from jax.sharding import PartitionSpec as P

HEAD_WIDTH = 128
QUERY_PER_KEY = 4
KEY_BLOCK = 256
LOG2E = 1.4426950408889634
NT = (((1,), (1,)), ((), ()))


EPSILON = 1e-06
THETA = 1000000.0


def rms_norm(values, gain):
    mean_square = jnp.mean(values * values, axis=-1, keepdims=True)
    return values * lax.rsqrt(mean_square + EPSILON) * gain


def rope_tables(positions, width):
    half = width // 2
    frequency = THETA ** (-2.0 * jnp.arange(half, dtype=jnp.float32) / width)
    angles = positions.astype(jnp.float32)[:, None] * frequency[None, :]
    return (jnp.cos(angles), jnp.sin(angles))


def rotate(values, cosine, sine):
    half = values.shape[-1] // 2
    layout = (cosine.shape[0],) + (1,) * (values.ndim - 2) + (half,)
    cosine = cosine.reshape(layout)
    sine = sine.reshape(layout)
    first = values[..., :half]
    second = values[..., half:]
    return jnp.concatenate(
        [first * cosine - second * sine, second * cosine + first * sine], axis=-1
    )


def attention_kernel(
    span_ref, q_ref, kv_ref, up_ref, bound_ref,
    context_ref, dq_ref, dkv_ref,
    exp_ref, q4_ref, up4_ref, num_ref, den_ref, dqt_ref,
):
    rows = q_ref.shape[0]
    width = HEAD_WIDTH
    block = KEY_BLOCK
    scale = width ** (-0.5)
    start_row = bound_ref[0:1, :]
    end_row = bound_ref[1:2, :]
    low, high = span_ref[0], span_ref[1]
    for g in range(QUERY_PER_KEY):
        q4_ref[g] = q_ref[:, g * width : (g + 1) * width]
    num_ref[...] = jnp.zeros_like(num_ref)
    den_ref[...] = jnp.zeros_like(den_ref)
    dqt_ref[...] = jnp.zeros_like(dqt_ref)
    dkv_ref[...] = jnp.zeros_like(dkv_ref)

    def forward(i, carry):
        at = pl.ds(pl.multiple_of(i * block, block), block)
        key = kv_ref[at, 0:width]
        value_t = kv_ref[at, width : 2 * width].T
        place = lax.broadcasted_iota(jnp.int32, (block, rows), 0) + i * block
        mask = (place >= start_row) & (place < end_row)
        for g in range(QUERY_PER_KEY):
            scores = lax.dot_general(
                key, q4_ref[g], NT, preferred_element_type=jnp.float32
            )
            exponent = jnp.where(mask, jnp.exp2(scores * (scale * LOG2E)), 0.0)
            den_ref[g] += jnp.sum(exponent.reshape(block // 8, 8, rows), axis=0)
            rounded = exponent.astype(jnp.bfloat16)
            exp_ref[g, at, :] = rounded
            num_ref[g] += jnp.dot(value_t, rounded, preferred_element_type=jnp.float32)
        return carry

    lax.fori_loop(low, high, forward, 0)
    corrections = []
    for g in range(QUERY_PER_KEY):
        columns = slice(g * width, (g + 1) * width)
        inverse = 1.0 / jnp.sum(den_ref[g], axis=0, keepdims=True)
        context_t = (num_ref[g] * inverse).astype(jnp.bfloat16).astype(jnp.float32)
        context_ref[:, columns] = context_t.T.astype(jnp.bfloat16)
        up_t = up_ref[:, columns].astype(jnp.float32).T
        up_t = (up_t * inverse).astype(jnp.bfloat16).astype(jnp.float32)
        up4_ref[g] = up_t.T.astype(jnp.bfloat16)
        corrections.append(jnp.sum(up_t * context_t, axis=0, keepdims=True))

    def backward(i, carry):
        at = pl.ds(pl.multiple_of(i * block, block), block)
        key_t = kv_ref[at, 0:width].T
        value = kv_ref[at, width : 2 * width]
        dk = jnp.zeros((block, width), jnp.float32)
        dv = jnp.zeros((block, width), jnp.float32)
        for g in range(QUERY_PER_KEY):
            grads = lax.dot_general(
                value, up4_ref[g], NT, preferred_element_type=jnp.float32
            )
            rounded = exp_ref[g, at, :]
            ds = (rounded.astype(jnp.float32) * (grads - corrections[g])).astype(jnp.bfloat16)
            dk += jnp.dot(ds, q4_ref[g], preferred_element_type=jnp.float32)
            dv += jnp.dot(rounded, up4_ref[g], preferred_element_type=jnp.float32)
            dqt_ref[g] += jnp.dot(key_t, ds, preferred_element_type=jnp.float32)
        dkv_ref[at, 0:width] = (dk * scale).astype(jnp.bfloat16)
        dkv_ref[at, width : 2 * width] = dv.astype(jnp.bfloat16)
        return carry

    lax.fori_loop(low, high, backward, 0)
    for g in range(QUERY_PER_KEY):
        dq_ref[:, g * width : (g + 1) * width] = (dqt_ref[g] * scale).T


def attention(span, queries, keys_values, upstream, bounds):
    rows = queries.shape[0]
    total = keys_values.shape[0]
    group = QUERY_PER_KEY
    vmem = pl.BlockSpec(memory_space=pltpu.VMEM)
    return pl.pallas_call(
        attention_kernel,
        out_shape=(
            jax.ShapeDtypeStruct((rows, group * HEAD_WIDTH), jnp.bfloat16),
            jax.ShapeDtypeStruct((rows, group * HEAD_WIDTH), jnp.float32),
            jax.ShapeDtypeStruct((total, 2 * HEAD_WIDTH), jnp.bfloat16),
        ),
        in_specs=[pl.BlockSpec(memory_space=pltpu.SMEM)] + [vmem] * 4,
        out_specs=(vmem, vmem, vmem),
        scratch_shapes=[
            pltpu.VMEM((group, total, rows), jnp.bfloat16),
            pltpu.VMEM((group, rows, HEAD_WIDTH), jnp.bfloat16),
            pltpu.VMEM((group, rows, HEAD_WIDTH), jnp.bfloat16),
            pltpu.VMEM((group, HEAD_WIDTH, rows), jnp.float32),
            pltpu.VMEM((group, 8, rows), jnp.float32),
            pltpu.VMEM((group, HEAD_WIDTH, rows), jnp.float32),
        ],
        compiler_params=pltpu.CompilerParams(vmem_limit_bytes=48 * 1024 * 1024),
        cost_estimate=pl.CostEstimate(
            flops=14 * group * rows * total * HEAD_WIDTH,
            bytes_accessed=8 * total * HEAD_WIDTH,
            transcendentals=group * rows * total,
        ),
    )(span, queries, keys_values, upstream, bounds)


def on_device(tokens, projection, norm_gain, query_gain, key_gain, segment_ids, context_cotangent):
    tokens_wide = tokens.astype(jnp.float32)
    normed_own = rms_norm(tokens_wide, norm_gain).astype(jnp.bfloat16)
    normed_values = lax.all_gather(normed_own, "tp", axis=0, tiled=True)
    local_tokens = normed_values.shape[0]
    column_count = projection.shape[1]
    groups = column_count // ((QUERY_PER_KEY + 2) * HEAD_WIDTH)
    offset = lax.axis_index("ctx") * local_tokens
    joined_rows = jnp.dot(
        normed_values,
        lax.all_gather(projection, "ctx", axis=0, tiled=True),
        preferred_element_type=jnp.float32,
    )
    joined_rows = joined_rows.reshape(local_tokens, groups, QUERY_PER_KEY + 2, HEAD_WIDTH)
    query_raw = joined_rows[:, :, :QUERY_PER_KEY, :]
    key_raw = joined_rows[:, :, QUERY_PER_KEY, :]
    value_raw = joined_rows[:, :, QUERY_PER_KEY + 1, :]
    positions = offset + jnp.arange(local_tokens, dtype=jnp.int32)
    cosine, sine = rope_tables(positions, HEAD_WIDTH)

    def head_map(raw, gain):
        return rotate(rms_norm(raw, gain), cosine, sine)

    queries = head_map(query_raw, query_gain).astype(jnp.bfloat16)
    keys = head_map(key_raw, key_gain).astype(jnp.bfloat16)
    values = value_raw.astype(jnp.bfloat16)
    query_segments = lax.dynamic_slice_in_dim(segment_ids, offset, local_tokens)
    starts = jnp.sum((segment_ids[None, :] < query_segments[:, None]).astype(jnp.int32), axis=1)
    ends = jnp.sum((segment_ids[None, :] <= query_segments[:, None]).astype(jnp.int32), axis=1)
    bounds = jnp.stack([starts, ends])
    span = jnp.stack([starts[0] // KEY_BLOCK, (ends[-1] + KEY_BLOCK - 1) // KEY_BLOCK])
    keys_values = lax.all_gather(
        jnp.concatenate([keys[:, 0], values[:, 0]], axis=1), "ctx", axis=0, tiled=True
    )
    context, query_grads, kv_grads = attention(
        span,
        queries.reshape(local_tokens, -1),
        keys_values,
        context_cotangent,
        bounds,
    )
    query_grads = query_grads.reshape(local_tokens, groups, QUERY_PER_KEY, HEAD_WIDTH)
    kv_grads = lax.psum_scatter(kv_grads, "ctx", scatter_dimension=0, tiled=True).astype(jnp.float32)
    key_grads = kv_grads[:, None, :HEAD_WIDTH]
    value_gradient = kv_grads[:, None, HEAD_WIDTH:]
    mapped, query_back = jax.vjp(head_map, query_raw, query_gain)
    unnormed_query_gradient, query_gain_term = query_back(query_grads)
    mapped, key_back = jax.vjp(head_map, key_raw, key_gain)
    unnormed_key_gradient, key_gain_term = key_back(key_grads)
    joined_gradient = (
        jnp.concatenate(
            [
                unnormed_query_gradient,
                unnormed_key_gradient[:, :, None, :],
                value_gradient[:, :, None, :],
            ],
            axis=2,
        )
        .reshape(local_tokens, column_count)
        .astype(jnp.bfloat16)
    )
    projection_grads = lax.psum_scatter(
        lax.dot_general(
            normed_values,
            joined_gradient,
            (((0,), (0,)), ((), ())),
            preferred_element_type=jnp.float32,
        ).astype(jnp.bfloat16),
        "ctx",
        scatter_dimension=0,
        tiled=True,
    ).astype(jnp.float32)
    normed_terms = lax.dot_general(
        joined_gradient,
        lax.all_gather(projection, "ctx", axis=0, tiled=True),
        (((1,), (1,)), ((), ())),
        preferred_element_type=jnp.float32,
    )
    normed_grads = lax.psum_scatter(
        normed_terms.astype(jnp.bfloat16), "tp", scatter_dimension=0, tiled=True
    ).astype(jnp.float32)
    mapped, norm_back = jax.vjp(rms_norm, tokens_wide, norm_gain)
    token_grads, norm_gain_term = norm_back(normed_grads)
    norm_gain_grads, query_gain_grads, key_gain_grads = lax.psum(
        (norm_gain_term, query_gain_term, key_gain_term), ("ctx", "tp")
    )
    return (
        context.reshape(local_tokens, groups * QUERY_PER_KEY * HEAD_WIDTH),
        token_grads,
        projection_grads,
        norm_gain_grads,
        query_gain_grads,
        key_gain_grads,
    )


def solution(mesh):
    placed = (
        P(("dp", "ctx", "tp"), None),
        P("ctx", "tp"),
        P(),
        P(),
        P(),
        P("dp"),
        P(("dp", "ctx"), "tp"),
    )
    return jax.shard_map(
        on_device,
        mesh=mesh,
        in_specs=placed,
        out_specs=(
            P(("dp", "ctx"), "tp"),
            P(("dp", "ctx", "tp"), None),
            P(("dp", "ctx"), "tp"),
            P("dp"),
            P("dp"),
            P("dp"),
        ),
        check_vma=False,
    )
```

```python
import jax
import jax.numpy as jnp
from jax import lax
from jax.experimental import pallas as pl
from jax.experimental.pallas import tpu as pltpu
from jax.sharding import PartitionSpec as P

HEAD_WIDTH = 128
QUERY_PER_KEY = 4
KEY_BLOCK = 256
SIDE = 4
EPSILON = 1e-06
THETA = 1000000.0
LOG2E = 1.4426950408889634
MESH = pl.DeviceIdType.MESH
NT = (((1,), (1,)), ((), ()))
TN = (((0,), (0,)), ((), ()))


def wrap(value):
    return lax.rem(value + 2 * SIDE, SIDE)


def part_of(step):
    return 0 if step == 1 else 1


class Torus:
    def __init__(self, send_sems, recv_sems):
        ctx, tp = lax.axis_index("ctx"), lax.axis_index("tp")
        self.place = {
            "y": lax.div(ctx, SIDE),
            "x": lax.rem(ctx, SIDE),
            "z": lax.div(tp, 2),
            "core": lax.rem(tp, 2),
        }
        self.tp = tp
        self.sems = (send_sems, recv_sems)
        self.sent = []

    def along(self, axis, step):
        at = self.place
        if axis == "x":
            return {"ctx": at["y"] * SIDE + wrap(at["x"] + step)}
        if axis == "y":
            return {"ctx": wrap(at["y"] + step) * SIDE + at["x"]}
        if axis == "z":
            return {"tp": wrap(at["z"] + step) * 2 + at["core"]}
        return {"tp": at["z"] * 2 + 1 - at["core"]}

    def greet(self, steps):
        barrier = pltpu.get_barrier_semaphore()
        partners = [(axis, step) for axis in ("x", "y", "z") for step in steps] + [("core", 1)]
        for axis, step in partners:
            pl.semaphore_signal(
                barrier, inc=1, device_id=self.along(axis, step), device_id_type=MESH
            )
        pl.semaphore_wait(barrier, len(partners))

    def copy(self, index, source, target, axis, step):
        return pltpu.make_async_remote_copy(
            src_ref=source,
            dst_ref=target,
            send_sem=self.sems[0].at[index],
            recv_sem=self.sems[1].at[index],
            device_id=self.along(axis, step),
            device_id_type=MESH,
        )

    def send(self, source, target, axis, step):
        index = len(self.sent)
        copy = self.copy(index, source, target, axis, step)
        copy.start()
        self.sent.append(copy)
        return index

    def arrive(self, index, target):
        self.copy(index, target, target, "core", 1).wait_recv()

    def close(self):
        for copy in self.sent:
            copy.wait_send()


class Blocks:
    def __init__(self, torus, data, orders):
        self.torus, self.data, self.orders = torus, data, orders
        self.rows = data.shape[0] // (SIDE * SIDE)
        self.keys = {}

    def at(self, half, first, second, part=None):
        offset = dict(zip(self.orders[half], (first, second)))
        place = self.torus.place
        block = wrap(place["y"] + offset["y"]) * SIDE + wrap(place["x"] + offset["x"])
        rows = self.rows
        start = block * rows + half * (rows // 2)
        if part is not None:
            start = start + part * (rows // 4)
        size = rows // 2 if part is None else rows // 4
        return self.data.at[pl.ds(pl.multiple_of(start, rows // 4), size), :]

    def send(self, key, source, target, axis, step):
        self.keys[key] = self.torus.send(source, target, axis, step)

    def arrive(self, key, target):
        self.torus.arrive(self.keys[key], target)


class Gather(Blocks):
    def __init__(self, torus, data):
        super().__init__(torus, data, (("x", "y"), ("y", "x")))

    def pass_on(self, half, first):
        for step in (1, -1):
            block = self.at(half, first, 0)
            self.send(("q", half, first, step), block, block, self.orders[half][1], step)

    def start(self):
        for half in (0, 1):
            for step in (1, -1):
                block = self.at(half, 0, 0)
                self.send(("p", half, step), block, block, self.orders[half][0], step)
        for half in (0, 1):
            self.pass_on(half, 0)

    def near(self):
        for half in (0, 1):
            for step in (1, -1):
                self.arrive(("p", half, step), self.at(half, -step, 0))
                block = self.at(half, -step, 0, part_of(step))
                self.send(("f", half, step), block, block, self.orders[half][0], step)
        for half in (0, 1):
            for step in (1, -1):
                self.pass_on(half, -step)

    def far(self):
        for half in (0, 1):
            for step in (1, -1):
                self.arrive(("f", half, step), self.at(half, 2, 0, part_of(step)))
            self.pass_on(half, 2)

    def cross(self, firsts):
        for first in firsts:
            for half in (0, 1):
                for step in (1, -1):
                    self.arrive(("q", half, first, step), self.at(half, first, -step))
                    block = self.at(half, first, -step, part_of(step))
                    self.send(("g", half, first, step), block, block, self.orders[half][1], step)

    def finish(self):
        for first in (0, -1, 1, 2):
            for half in (0, 1):
                for step in (1, -1):
                    self.arrive(("g", half, first, step), self.at(half, first, 2, part_of(step)))


def add_to(target, *sources):
    total = target[...].astype(jnp.float32)
    for source in sources:
        total = total + source[...].astype(jnp.float32)
    target[...] = total.astype(target.dtype)


class Scatter(Blocks):
    def __init__(self, torus, data, far_one, near_one, far_two, near_two):
        super().__init__(torus, data, (("y", "x"), ("x", "y")))
        self.far_one, self.near_one = far_one, near_one
        self.far_two, self.near_two = far_two, near_two

    def start(self, seconds=(2, 1, -1, 0)):
        for second in seconds:
            for half in (0, 1):
                for step in (1, -1):
                    self.send(
                        ("f1", half, second, step),
                        self.at(half, 2, second, part_of(step)),
                        self.far_one.at[half, second % SIDE, part_of(step)],
                        self.orders[half][0],
                        step,
                    )

    def turn(self, seconds=(2, 1, -1, 0)):
        for second in seconds:
            for half in (0, 1):
                for step in (1, -1):
                    landed = self.far_one.at[half, second % SIDE, part_of(step)]
                    self.arrive(("f1", half, second, step), landed)
                    add_to(self.at(half, step, second, part_of(step)), landed)
                    self.send(
                        ("n1", half, second, step),
                        self.at(half, step, second),
                        self.near_one.at[half, second % SIDE, part_of(step)],
                        self.orders[half][0],
                        step,
                    )

    def land(self, seconds=(2, 1, -1, 0)):
        for second in seconds:
            for half in (0, 1):
                landed = [self.near_one.at[half, second % SIDE, part] for part in (0, 1)]
                for step in (1, -1):
                    self.arrive(("n1", half, second, step), landed[part_of(step)])
                add_to(self.at(half, 0, second), *landed)
                if second == 2:
                    for step in (1, -1):
                        self.send(
                            ("f2", half, step),
                            self.at(half, 0, 2, part_of(step)),
                            self.far_two.at[half, part_of(step)],
                            self.orders[half][1],
                            step,
                        )

    def turn_two(self):
        for half in (0, 1):
            for step in (1, -1):
                landed = self.far_two.at[half, part_of(step)]
                self.arrive(("f2", half, step), landed)
                add_to(self.at(half, 0, step, part_of(step)), landed)
                self.send(
                    ("n2", half, step),
                    self.at(half, 0, step),
                    self.near_two.at[half, part_of(step)],
                    self.orders[half][1],
                    step,
                )

    def finish(self, store):
        for half in (0, 1):
            landed = [self.near_two.at[half, part] for part in (0, 1)]
            for step in (1, -1):
                self.arrive(("n2", half, step), landed[part_of(step)])
            total = self.at(half, 0, 0)[...].astype(jnp.float32)
            for source in landed:
                total = total + source[...].astype(jnp.float32)
            store(slice(half * (self.rows // 2), (half + 1) * (self.rows // 2)), total)


def scatter_scratch(rows, columns):
    return [
        pltpu.VMEM((2, SIDE, 2, rows // 4, columns), jnp.bfloat16),
        pltpu.VMEM((2, SIDE, 2, rows // 2, columns), jnp.bfloat16),
        pltpu.VMEM((2, 2, rows // 4, columns), jnp.bfloat16),
        pltpu.VMEM((2, 2, rows // 2, columns), jnp.bfloat16),
    ]


def inverse_rms(values):
    return lax.rsqrt(jnp.mean(values * values, axis=-1, keepdims=True) + EPSILON)


def turn_halves(values):
    return pltpu.roll(values, HEAD_WIDTH // 2, 1)


def head_map(raw, gain, cosine, sine):
    scaled = raw * inverse_rms(raw) * gain
    return scaled * cosine + turn_halves(scaled) * sine


def head_map_back(raw, gain, cosine, sine, grads):
    inverse = inverse_rms(raw)
    unit = raw * inverse
    turned = grads * cosine + turn_halves(grads * sine)
    gain_grads = jnp.sum(turned * unit, axis=0, keepdims=True)
    scaled = turned * gain
    raw_grads = inverse * (scaled - unit * jnp.mean(scaled * unit, axis=-1, keepdims=True))
    return raw_grads, gain_grads


def project_kernel(
    tokens_ref, shard_ref, norm_gain_ref, query_gain_ref, key_gain_ref, cosine_ref, sine_ref,
    q_ref, kv_ref, raw_ref, normed_ref, wkv_ref, wq_ref,
    send_sems, recv_sems,
):
    width = HEAD_WIDTH
    split = QUERY_PER_KEY * width
    torus = Torus(send_sems, recv_sems)
    torus.greet((1, -1))
    rows = shard_ref.shape[0]
    ctx = lax.axis_index("ctx")
    own = pl.ds(pl.multiple_of(ctx * rows, rows), rows)
    wkv_ref[own, :] = shard_ref[:, split:]
    weights_kv = Gather(torus, wkv_ref)
    weights_kv.start()

    count = tokens_ref.shape[0]

    def token_rows(step, part=None, flip=False):
        core = torus.place["core"]
        index = wrap(torus.place["z"] + step) * 2 + (1 - core if flip else core)
        size = count if part is None else count // 2
        start = index * count + (0 if part is None else part * (count // 2))
        return normed_ref.at[pl.ds(pl.multiple_of(start, count // 2), size), :]

    tokens = tokens_ref[...].astype(jnp.float32)
    token_rows(0)[...] = (tokens * inverse_rms(tokens) * norm_gain_ref[...]).astype(jnp.bfloat16)
    mine = token_rows(0)
    ring = {step: torus.send(mine, mine, "z", step) for step in (1, -1)}
    pair = {0: torus.send(mine, mine, "core", 1)}

    wq_ref[own, :] = shard_ref[:, :split]
    weights_q = Gather(torus, wq_ref)
    weights_kv.near()
    weights_q.start()
    onward = {}
    for step in (1, -1):
        torus.arrive(ring[step], token_rows(-step))
        piece = token_rows(-step, part_of(step))
        onward[step] = torus.send(piece, piece, "z", step)
        block = token_rows(-step)
        pair[-step] = torus.send(block, block, "core", 1)
    weights_kv.far()
    for step in (1, -1):
        torus.arrive(onward[step], token_rows(2, part_of(step)))
    block = token_rows(2)
    pair[2] = torus.send(block, block, "core", 1)
    weights_kv.cross((0, -1, 1))
    weights_q.near()
    weights_kv.cross((2,))
    weights_q.far()
    for step in (0, -1, 1, 2):
        torus.arrive(pair[step], token_rows(step, flip=True))
    weights_kv.finish()

    cosine, sine = cosine_ref[...], sine_ref[...]
    raw = jnp.dot(normed_ref[...], wkv_ref[...], preferred_element_type=jnp.float32)
    raw_ref[:, split:] = raw[:, :width]
    kv_ref[own, 0:width] = head_map(raw[:, :width], key_gain_ref[...], cosine, sine).astype(
        jnp.bfloat16
    )
    kv_ref[own, width:] = raw[:, width:].astype(jnp.bfloat16)
    keys_values = Gather(torus, kv_ref)
    keys_values.start()
    weights_q.cross((0, -1, 1))
    keys_values.near()
    weights_q.cross((2,))
    keys_values.far()
    weights_q.finish()
    keys_values.cross((0, -1, 1, 2))

    raw = jnp.dot(normed_ref[...], wq_ref[...], preferred_element_type=jnp.float32)
    raw_ref[:, :split] = raw
    for g in range(QUERY_PER_KEY):
        columns = slice(g * width, (g + 1) * width)
        q_ref[:, columns] = head_map(raw[:, columns], query_gain_ref[...], cosine, sine).astype(
            jnp.bfloat16
        )
    keys_values.finish()
    torus.close()


def project(tokens, shard, norm_gain, query_gain, key_gain, cosine, sine):
    rows, columns = shard.shape
    count, depth = tokens.shape
    local = cosine.shape[0]
    total = local * SIDE * SIDE
    width = HEAD_WIDTH
    split = QUERY_PER_KEY * width
    vmem = pl.BlockSpec(memory_space=pltpu.VMEM)
    copies = 3 * 40 + 8
    return pl.pallas_call(
        project_kernel,
        out_shape=(
            jax.ShapeDtypeStruct((local, split), jnp.bfloat16),
            jax.ShapeDtypeStruct((total, 2 * width), jnp.bfloat16),
            jax.ShapeDtypeStruct((local, split + width), jnp.float32),
            jax.ShapeDtypeStruct((local, depth), jnp.bfloat16),
            jax.ShapeDtypeStruct((depth, 2 * width), jnp.bfloat16),
            jax.ShapeDtypeStruct((depth, split), jnp.bfloat16),
        ),
        in_specs=[vmem] * 7,
        out_specs=(vmem,) * 6,
        scratch_shapes=[pltpu.SemaphoreType.DMA((copies,)), pltpu.SemaphoreType.DMA((copies,))],
        compiler_params=pltpu.CompilerParams(
            collective_id=0, has_side_effects=True, vmem_limit_bytes=48 * 1024 * 1024
        ),
        cost_estimate=pl.CostEstimate(
            flops=2 * local * depth * columns, bytes_accessed=2 * depth * columns, transcendentals=0
        ),
    )(tokens, shard, norm_gain, query_gain, key_gain, cosine, sine)


def attention_kernel(
    span_ref, q_ref, kv_ref, up_ref, bound_ref,
    context_ref, dq_ref, dkv_ref,
    exp_ref, q4_ref, up4_ref, num_ref, den_ref, dqt_ref,
):
    rows = q_ref.shape[0]
    width = HEAD_WIDTH
    block = KEY_BLOCK
    scale = width ** (-0.5)
    start_row = bound_ref[0:1, :]
    end_row = bound_ref[1:2, :]
    low, high = span_ref[0], span_ref[1]
    for g in range(QUERY_PER_KEY):
        q4_ref[g] = q_ref[:, g * width : (g + 1) * width]
    num_ref[...] = jnp.zeros_like(num_ref)
    den_ref[...] = jnp.zeros_like(den_ref)
    dqt_ref[...] = jnp.zeros_like(dqt_ref)
    dkv_ref[...] = jnp.zeros_like(dkv_ref)

    def forward(i, carry):
        at = pl.ds(pl.multiple_of(i * block, block), block)
        key = kv_ref[at, 0:width]
        value_t = kv_ref[at, width : 2 * width].T
        place = lax.broadcasted_iota(jnp.int32, (block, rows), 0) + i * block
        mask = (place >= start_row) & (place < end_row)
        for g in range(QUERY_PER_KEY):
            scores = lax.dot_general(
                key, q4_ref[g], NT, preferred_element_type=jnp.float32
            )
            exponent = jnp.where(mask, jnp.exp2(scores * (scale * LOG2E)), 0.0)
            den_ref[g] += jnp.sum(exponent.reshape(block // 8, 8, rows), axis=0)
            rounded = exponent.astype(jnp.bfloat16)
            exp_ref[g, at, :] = rounded
            num_ref[g] += jnp.dot(value_t, rounded, preferred_element_type=jnp.float32)
        return carry

    lax.fori_loop(low, high, forward, 0)
    corrections = []
    for g in range(QUERY_PER_KEY):
        columns = slice(g * width, (g + 1) * width)
        inverse = 1.0 / jnp.sum(den_ref[g], axis=0, keepdims=True)
        context_t = (num_ref[g] * inverse).astype(jnp.bfloat16).astype(jnp.float32)
        context_ref[:, columns] = context_t.T.astype(jnp.bfloat16)
        up_t = up_ref[:, columns].astype(jnp.float32).T
        up_t = (up_t * inverse).astype(jnp.bfloat16).astype(jnp.float32)
        up4_ref[g] = up_t.T.astype(jnp.bfloat16)
        corrections.append(jnp.sum(up_t * context_t, axis=0, keepdims=True))

    def backward(i, carry):
        at = pl.ds(pl.multiple_of(i * block, block), block)
        key_t = kv_ref[at, 0:width].T
        value = kv_ref[at, width : 2 * width]
        dk = jnp.zeros((block, width), jnp.float32)
        dv = jnp.zeros((block, width), jnp.float32)
        for g in range(QUERY_PER_KEY):
            grads = lax.dot_general(
                value, up4_ref[g], NT, preferred_element_type=jnp.float32
            )
            rounded = exp_ref[g, at, :]
            ds = (rounded.astype(jnp.float32) * (grads - corrections[g])).astype(jnp.bfloat16)
            dk += jnp.dot(ds, q4_ref[g], preferred_element_type=jnp.float32)
            dv += jnp.dot(rounded, up4_ref[g], preferred_element_type=jnp.float32)
            dqt_ref[g] += jnp.dot(key_t, ds, preferred_element_type=jnp.float32)
        dkv_ref[at, 0:width] = (dk * scale).astype(jnp.bfloat16)
        dkv_ref[at, width : 2 * width] = dv.astype(jnp.bfloat16)
        return carry

    lax.fori_loop(low, high, backward, 0)
    for g in range(QUERY_PER_KEY):
        dq_ref[:, g * width : (g + 1) * width] = (dqt_ref[g] * scale).T


def attention(span, queries, keys_values, upstream, bounds):
    rows = queries.shape[0]
    total = keys_values.shape[0]
    group = QUERY_PER_KEY
    vmem = pl.BlockSpec(memory_space=pltpu.VMEM)
    return pl.pallas_call(
        attention_kernel,
        out_shape=(
            jax.ShapeDtypeStruct((rows, group * HEAD_WIDTH), jnp.bfloat16),
            jax.ShapeDtypeStruct((rows, group * HEAD_WIDTH), jnp.float32),
            jax.ShapeDtypeStruct((total, 2 * HEAD_WIDTH), jnp.bfloat16),
        ),
        in_specs=[pl.BlockSpec(memory_space=pltpu.SMEM)] + [vmem] * 4,
        out_specs=(vmem, vmem, vmem),
        scratch_shapes=[
            pltpu.VMEM((group, total, rows), jnp.bfloat16),
            pltpu.VMEM((group, rows, HEAD_WIDTH), jnp.bfloat16),
            pltpu.VMEM((group, rows, HEAD_WIDTH), jnp.bfloat16),
            pltpu.VMEM((group, HEAD_WIDTH, rows), jnp.float32),
            pltpu.VMEM((group, 8, rows), jnp.float32),
            pltpu.VMEM((group, HEAD_WIDTH, rows), jnp.float32),
        ],
        compiler_params=pltpu.CompilerParams(vmem_limit_bytes=48 * 1024 * 1024),
        cost_estimate=pl.CostEstimate(
            flops=14 * group * rows * total * HEAD_WIDTH,
            bytes_accessed=8 * total * HEAD_WIDTH,
            transcendentals=group * rows * total,
        ),
    )(span, queries, keys_values, upstream, bounds)


def gradient_kernel(
    dq_ref, dkv_hbm, raw_ref, normed_hbm, wq_hbm, wkv_hbm, tokens_ref,
    norm_gain_ref, query_gain_ref, key_gain_ref, cosine_ref, sine_ref,
    token_grads_ref, projection_grads_ref, gains_ref,
    send_sems, recv_sems, local_sems,
    dkv_ref, normed_ref, wq_ref, wkv_ref, jq_ref, jkv_ref, gq_ref, gkv_ref, dkv_sum_ref,
    terms_ref, pair_ref, zfar_ref, znear_ref, gx_ref, gy_ref, gz_ref, gc_ref,
    *boxes,
):
    width = HEAD_WIDTH
    split = QUERY_PER_KEY * width
    torus = Torus(send_sems, recv_sems)
    loads = [
        pltpu.make_async_copy(source, target, local_sems.at[i])
        for i, (source, target) in enumerate(
            ((dkv_hbm, dkv_ref), (normed_hbm, normed_ref), (wq_hbm, wq_ref), (wkv_hbm, wkv_ref))
        )
    ]
    for load in loads:
        load.start()
    torus.greet((1, 2, 3))
    loads[0].wait()
    dkv = Scatter(torus, dkv_ref, *boxes[0:4])
    dwq = Scatter(torus, gq_ref, *boxes[4:8])
    dwkv = Scatter(torus, gkv_ref, *boxes[8:12])
    dkv.start()

    cosine, sine = cosine_ref[...], sine_ref[...]
    query_gain_grads = jnp.zeros((1, width), jnp.float32)
    for g in range(QUERY_PER_KEY):
        columns = slice(g * width, (g + 1) * width)
        raw_grads, gain_grads = head_map_back(
            raw_ref[:, columns], query_gain_ref[...], cosine, sine, dq_ref[:, columns]
        )
        jq_ref[:, columns] = raw_grads.astype(jnp.bfloat16)
        query_gain_grads = query_gain_grads + gain_grads
    loads[1].wait()

    def weight_grads(j_ref, g_ref):
        def body(i, carry):
            at = pl.ds(pl.multiple_of(i * 256, 256), 256)
            g_ref[at, :] = lax.dot_general(
                normed_ref[:, at], j_ref[...], TN, preferred_element_type=jnp.float32
            ).astype(jnp.bfloat16)
            return carry

        lax.fori_loop(0, normed_ref.shape[1] // 256, body, 0)

    weight_grads(jq_ref, gq_ref)
    dkv.turn()
    dwq.start()
    dkv.land()
    dkv.turn_two()
    dwq.turn((2, 1))

    def keep_dkv(at, total):
        dkv_sum_ref[at, :] = total

    dkv.finish(keep_dkv)
    raw_grads, key_gain_grads = head_map_back(
        raw_ref[:, split:], key_gain_ref[...], cosine, sine, dkv_sum_ref[:, :width]
    )
    jkv_ref[:, :width] = raw_grads.astype(jnp.bfloat16)
    jkv_ref[:, width:] = dkv_sum_ref[:, width:].astype(jnp.bfloat16)
    weight_grads(jkv_ref, gkv_ref)
    dwkv.start()
    dwq.turn((-1, 0))
    loads[2].wait()
    loads[3].wait()

    def input_terms(i, carry):
        at = pl.ds(pl.multiple_of(i * 256, 256), 256)
        terms_ref[:, at] = (
            lax.dot_general(jq_ref[...], wq_ref[at, :], NT, preferred_element_type=jnp.float32)
            + lax.dot_general(jkv_ref[...], wkv_ref[at, :], NT, preferred_element_type=jnp.float32)
        ).astype(jnp.bfloat16)
        return carry

    lax.fori_loop(0, terms_ref.shape[1] // 256, input_terms, 0)

    count = tokens_ref.shape[0]

    def term_rows(step, part=None, flip=False):
        core = torus.place["core"]
        index = wrap(torus.place["z"] + step) * 2 + (1 - core if flip else core)
        size = count if part is None else count // 2
        start = index * count + (0 if part is None else part * (count // 2))
        return terms_ref.at[pl.ds(pl.multiple_of(start, count // 2), size), :]

    pair = {
        step: torus.send(term_rows(step, flip=True), pair_ref.at[step % SIDE], "core", 1)
        for step in (2, 1, -1, 0)
    }
    dwq.land((2,))
    dwkv.turn((2,))
    far = {}
    torus.arrive(pair[2], pair_ref.at[2])
    add_to(term_rows(2), pair_ref.at[2])
    for step in (1, -1):
        far[step] = torus.send(
            term_rows(2, part_of(step)), zfar_ref.at[part_of(step)], "z", step
        )
    dwq.land((1, -1))
    dwq.turn_two()
    near = {}
    for step in (1, -1):
        torus.arrive(pair[step], pair_ref.at[step % SIDE])
        add_to(term_rows(step), pair_ref.at[step % SIDE])
        torus.arrive(far[step], zfar_ref.at[part_of(step)])
        add_to(term_rows(step, part_of(step)), zfar_ref.at[part_of(step)])
        near[step] = torus.send(term_rows(step), znear_ref.at[part_of(step)], "z", step)
    dwkv.turn((1, -1, 0))
    dwq.land((0,))
    torus.arrive(pair[0], pair_ref.at[0])
    for step in (1, -1):
        torus.arrive(near[step], znear_ref.at[part_of(step)])
    normed_grads = term_rows(0)[...].astype(jnp.float32) + pair_ref[0].astype(jnp.float32)
    normed_grads = normed_grads + (
        znear_ref[0].astype(jnp.float32) + znear_ref[1].astype(jnp.float32)
    )
    tokens = tokens_ref[...].astype(jnp.float32)
    inverse = inverse_rms(tokens)
    unit = tokens * inverse
    norm_gain_grads = jnp.sum(normed_grads * unit, axis=0, keepdims=True)
    scaled = normed_grads * norm_gain_ref[...]
    token_grads_ref[...] = inverse * (
        scaled - unit * jnp.mean(scaled * unit, axis=-1, keepdims=True)
    )
    lines, columns = gains_ref.shape
    run = tokens.shape[1] // lines
    gains_ref[...] = jnp.zeros_like(gains_ref)
    for i in range(lines):
        gains_ref[i : i + 1, 0:run] = norm_gain_grads[:, i * run : (i + 1) * run]
    gains_ref[0:1, run:] = query_gain_grads
    gains_ref[1:2, run:] = key_gain_grads

    def share(axis, box):
        place, size = torus.place[axis], box.shape[0]
        box[place] = gains_ref[...]
        return [
            torus.send(box.at[place], box.at[place], axis, step) for step in range(1, size)
        ]

    def collect(axis, box, sent):
        place, size = torus.place[axis], box.shape[0]
        for step in range(1, size):
            torus.arrive(sent[step - 1], box.at[lax.rem(place + size - step, size)])
        total = box[0]
        for i in range(1, size):
            total = total + box[i]
        gains_ref[...] = total

    def keep_q(at, total):
        projection_grads_ref[at, :split] = total

    def keep_kv(at, total):
        projection_grads_ref[at, split:] = total

    sent = share("z", gz_ref)
    dwkv.land((2, 1))
    collect("z", gz_ref, sent)
    sent = share("core", gc_ref)
    dwkv.land((-1,))
    collect("core", gc_ref, sent)
    sent = share("x", gx_ref)
    dwkv.turn_two()
    dwq.finish(keep_q)
    collect("x", gx_ref, sent)
    sent = share("y", gy_ref)
    dwkv.land((0,))
    dwkv.finish(keep_kv)
    collect("y", gy_ref, sent)
    torus.close()


def gradients(
    dq, dkv, raw, normed, wq, wkv, tokens, norm_gain, query_gain, key_gain, cosine, sine
):
    local, depth = normed.shape
    count = tokens.shape[0]
    total = dkv.shape[0]
    width = HEAD_WIDTH
    split = QUERY_PER_KEY * width
    rows = depth // (SIDE * SIDE)
    lines = 8
    gains = (lines, depth // lines + width)
    vmem = pl.BlockSpec(memory_space=pltpu.VMEM)
    anywhere = pl.BlockSpec(memory_space=pl.ANY)
    copies = 3 * 40 + 8 + 10
    bf16, f32 = jnp.bfloat16, jnp.float32
    return pl.pallas_call(
        gradient_kernel,
        out_shape=(
            jax.ShapeDtypeStruct((count, depth), f32),
            jax.ShapeDtypeStruct((rows, split + 2 * width), f32),
            jax.ShapeDtypeStruct(gains, f32),
        ),
        in_specs=[vmem, anywhere, vmem, anywhere, anywhere, anywhere] + [vmem] * 6,
        out_specs=(vmem,) * 3,
        scratch_shapes=[
            pltpu.SemaphoreType.DMA((copies,)),
            pltpu.SemaphoreType.DMA((copies,)),
            pltpu.SemaphoreType.DMA((4,)),
            pltpu.VMEM((total, 2 * width), bf16),
            pltpu.VMEM((local, depth), bf16),
            pltpu.VMEM((depth, split), bf16),
            pltpu.VMEM((depth, 2 * width), bf16),
            pltpu.VMEM((local, split), bf16),
            pltpu.VMEM((local, 2 * width), bf16),
            pltpu.VMEM((depth, split), bf16),
            pltpu.VMEM((depth, 2 * width), bf16),
            pltpu.VMEM((local, 2 * width), f32),
            pltpu.VMEM((local, depth), bf16),
            pltpu.VMEM((SIDE, count, depth), bf16),
            pltpu.VMEM((2, count // 2, depth), bf16),
            pltpu.VMEM((2, count, depth), bf16),
            pltpu.VMEM((SIDE,) + gains, f32),
            pltpu.VMEM((SIDE,) + gains, f32),
            pltpu.VMEM((SIDE,) + gains, f32),
            pltpu.VMEM((2,) + gains, f32),
        ]
        + scatter_scratch(total // (SIDE * SIDE), 2 * width)
        + scatter_scratch(rows, split)
        + scatter_scratch(rows, 2 * width),
        compiler_params=pltpu.CompilerParams(
            collective_id=1, has_side_effects=True, vmem_limit_bytes=56 * 1024 * 1024
        ),
        cost_estimate=pl.CostEstimate(
            flops=4 * local * depth * (split + 2 * width),
            bytes_accessed=4 * depth * (split + 2 * width),
            transcendentals=0,
        ),
    )(dq, dkv, raw, normed, wq, wkv, tokens, norm_gain, query_gain, key_gain, cosine, sine)


def rope_tables(positions, width):
    half = width // 2
    frequency = THETA ** (-2.0 * jnp.arange(half, dtype=jnp.float32) / width)
    angles = positions.astype(jnp.float32)[:, None] * frequency[None, :]
    cosine, sine = jnp.cos(angles), jnp.sin(angles)
    return (
        jnp.concatenate([cosine, cosine], axis=1),
        jnp.concatenate([-sine, sine], axis=1),
    )


def on_device(tokens, projection, norm_gain, query_gain, key_gain, segment_ids, context_cotangent):
    local = context_cotangent.shape[0]
    offset = lax.axis_index("ctx") * local
    positions = offset + jnp.arange(local, dtype=jnp.int32)
    cosine, sine = rope_tables(positions, HEAD_WIDTH)
    norm_gain = norm_gain.reshape(1, -1)
    query_gain = query_gain.reshape(1, -1)
    key_gain = key_gain.reshape(1, -1)
    query_segments = lax.dynamic_slice_in_dim(segment_ids, offset, local)
    starts = jnp.sum((segment_ids[:, None] < query_segments[None, :]).astype(jnp.int32), axis=0)
    ends = jnp.sum((segment_ids[:, None] <= query_segments[None, :]).astype(jnp.int32), axis=0)
    bounds = jnp.stack([starts, ends])
    span = jnp.stack([starts[0] // KEY_BLOCK, (ends[-1] + KEY_BLOCK - 1) // KEY_BLOCK])
    queries, keys_values, raw, normed, wkv, wq = project(
        tokens, projection, norm_gain, query_gain, key_gain, cosine, sine
    )
    context, query_grads, kv_grads = attention(
        span, queries, keys_values, context_cotangent, bounds
    )
    token_grads, projection_grads, gains = gradients(
        query_grads, kv_grads, raw, normed, wq, wkv, tokens,
        norm_gain, query_gain, key_gain, cosine, sine,
    )
    run = gains.shape[1] - HEAD_WIDTH
    return (
        context,
        token_grads,
        projection_grads,
        gains[:, :run].reshape(-1),
        gains[0, run:],
        gains[1, run:],
    )


def solution(mesh):
    placed = (
        P(("dp", "ctx", "tp"), None),
        P("ctx", "tp"),
        P(),
        P(),
        P(),
        P("dp"),
        P(("dp", "ctx"), "tp"),
    )
    return jax.shard_map(
        on_device,
        mesh=mesh,
        in_specs=placed,
        out_specs=(
            P(("dp", "ctx"), "tp"),
            P(("dp", "ctx", "tp"), None),
            P(("dp", "ctx"), "tp"),
            P("dp"),
            P("dp"),
            P("dp"),
        ),
        check_vma=False,
    )
```

```python
import jax
import jax.numpy as jnp
import numpy as np
from jax import lax
from jax.experimental import pallas as pl
from jax.experimental.pallas import tpu as pltpu
from jax.sharding import PartitionSpec as P

HEAD_WIDTH = 128
QUERY_PER_KEY = 4
KEY_BLOCK = 512
ALIGN = 16
SEGMENTS = 16
SIDE = 4
EPSILON = 1e-06
THETA = 1000000.0
LOG2E = 1.4426950408889634
MESH = pl.DeviceIdType.MESH
NT = (((1,), (1,)), ((), ()))
TN = (((0,), (0,)), ((), ()))


def wrap(value):
    return lax.rem(value + 2 * SIDE, SIDE)


def part_of(step):
    return 0 if step == 1 else 1


class Torus:
    def __init__(self, send_sems, recv_sems):
        ctx, tp = lax.axis_index("ctx"), lax.axis_index("tp")
        self.place = {
            "y": lax.div(ctx, SIDE),
            "x": lax.rem(ctx, SIDE),
            "z": lax.div(tp, 2),
            "core": lax.rem(tp, 2),
        }
        self.tp = tp
        self.sems = (send_sems, recv_sems)
        self.sent = []

    def along(self, axis, step):
        at = self.place
        if axis == "x":
            return {"ctx": at["y"] * SIDE + wrap(at["x"] + step)}
        if axis == "y":
            return {"ctx": wrap(at["y"] + step) * SIDE + at["x"]}
        if axis == "z":
            return {"tp": wrap(at["z"] + step) * 2 + at["core"]}
        return {"tp": at["z"] * 2 + 1 - at["core"]}

    def greet(self, steps):
        barrier = pltpu.get_barrier_semaphore()
        partners = [(axis, step) for axis in ("x", "y", "z") for step in steps] + [("core", 1)]
        for axis, step in partners:
            pl.semaphore_signal(
                barrier, inc=1, device_id=self.along(axis, step), device_id_type=MESH
            )
        pl.semaphore_wait(barrier, len(partners))

    def copy(self, index, source, target, axis, step):
        return pltpu.make_async_remote_copy(
            src_ref=source,
            dst_ref=target,
            send_sem=self.sems[0].at[index],
            recv_sem=self.sems[1].at[index],
            device_id=self.along(axis, step),
            device_id_type=MESH,
        )

    def send(self, source, target, axis, step):
        index = len(self.sent)
        copy = self.copy(index, source, target, axis, step)
        copy.start()
        self.sent.append(copy)
        return index

    def arrive(self, index, target):
        self.copy(index, target, target, "core", 1).wait_recv()

    def close(self):
        for copy in self.sent:
            copy.wait_send()


class Blocks:
    def __init__(self, torus, data, orders):
        self.torus, self.data, self.orders = torus, data, orders
        self.rows = data.shape[0] // (SIDE * SIDE)
        self.keys = {}

    def at(self, half, first, second, part=None, data=None):
        offset = dict(zip(self.orders[half], (first, second)))
        place = self.torus.place
        block = wrap(place["y"] + offset["y"]) * SIDE + wrap(place["x"] + offset["x"])
        rows = self.rows
        start = block * rows + half * (rows // 2)
        if part is not None:
            start = start + part * (rows // 4)
        size = rows // 2 if part is None else rows // 4
        data = self.data if data is None else data
        return data.at[pl.ds(pl.multiple_of(start, rows // 4), size), :]

    def send(self, key, source, target, axis, step):
        self.keys[key] = self.torus.send(source, target, axis, step)

    def arrive(self, key, target):
        self.torus.arrive(self.keys[key], target)


class Gather(Blocks):
    def __init__(self, torus, data):
        super().__init__(torus, data, (("x", "y"), ("y", "x")))

    def pass_on(self, half, first):
        for step in (1, -1):
            block = self.at(half, first, 0)
            self.send(("q", half, first, step), block, block, self.orders[half][1], step)

    def start(self):
        for half in (0, 1):
            for step in (1, -1):
                block = self.at(half, 0, 0)
                self.send(("p", half, step), block, block, self.orders[half][0], step)
        for half in (0, 1):
            self.pass_on(half, 0)

    def near(self):
        for half in (0, 1):
            for step in (1, -1):
                self.arrive(("p", half, step), self.at(half, -step, 0))
                block = self.at(half, -step, 0, part_of(step))
                self.send(("f", half, step), block, block, self.orders[half][0], step)
        for half in (0, 1):
            for step in (1, -1):
                self.pass_on(half, -step)

    def far(self):
        for half in (0, 1):
            for step in (1, -1):
                self.arrive(("f", half, step), self.at(half, 2, 0, part_of(step)))
            self.pass_on(half, 2)

    def cross(self, firsts):
        for first in firsts:
            for half in (0, 1):
                for step in (1, -1):
                    self.arrive(("q", half, first, step), self.at(half, first, -step))
                    block = self.at(half, first, -step, part_of(step))
                    self.send(("g", half, first, step), block, block, self.orders[half][1], step)

    def finish(self):
        for first in (0, -1, 1, 2):
            for half in (0, 1):
                for step in (1, -1):
                    self.arrive(("g", half, first, step), self.at(half, first, 2, part_of(step)))


def add_to(target, *sources):
    total = target[...].astype(jnp.float32)
    for source in sources:
        total = total + source[...].astype(jnp.float32)
    target[...] = total.astype(target.dtype)


class Scatter(Blocks):
    def __init__(self, torus, data, far_one, near_one, far_two, near_two):
        super().__init__(torus, data, (("y", "x"), ("x", "y")))
        self.far_one, self.near_one = far_one, near_one
        self.far_two, self.near_two = far_two, near_two

    def start(self, data=None):
        for second in (2, 1, -1, 0):
            for half in (0, 1):
                for step in (1, -1):
                    self.send(
                        ("f1", half, second, step),
                        self.at(half, 2, second, part_of(step), data),
                        self.far_one.at[half, second % SIDE, part_of(step)],
                        self.orders[half][0],
                        step,
                    )

    def turn(self, seconds=(2, 1, -1, 0)):
        for second in seconds:
            for half in (0, 1):
                for step in (1, -1):
                    landed = self.far_one.at[half, second % SIDE, part_of(step)]
                    self.arrive(("f1", half, second, step), landed)
                    add_to(self.at(half, step, second, part_of(step)), landed)
                    self.send(
                        ("n1", half, second, step),
                        self.at(half, step, second),
                        self.near_one.at[half, second % SIDE, part_of(step)],
                        self.orders[half][0],
                        step,
                    )

    def land(self, seconds=(2, 1, -1, 0)):
        for second in seconds:
            for half in (0, 1):
                landed = [self.near_one.at[half, second % SIDE, part] for part in (0, 1)]
                for step in (1, -1):
                    self.arrive(("n1", half, second, step), landed[part_of(step)])
                add_to(self.at(half, 0, second), *landed)
                if second == 2:
                    for step in (1, -1):
                        self.send(
                            ("f2", half, step),
                            self.at(half, 0, 2, part_of(step)),
                            self.far_two.at[half, part_of(step)],
                            self.orders[half][1],
                            step,
                        )

    def turn_two(self):
        for half in (0, 1):
            for step in (1, -1):
                landed = self.far_two.at[half, part_of(step)]
                self.arrive(("f2", half, step), landed)
                add_to(self.at(half, 0, step, part_of(step)), landed)
                self.send(
                    ("n2", half, step),
                    self.at(half, 0, step),
                    self.near_two.at[half, part_of(step)],
                    self.orders[half][1],
                    step,
                )

    def finish(self, store):
        for half in (0, 1):
            landed = [self.near_two.at[half, part] for part in (0, 1)]
            for step in (1, -1):
                self.arrive(("n2", half, step), landed[part_of(step)])
            total = self.at(half, 0, 0)[...].astype(jnp.float32)
            for source in landed:
                total = total + source[...].astype(jnp.float32)
            store(slice(half * (self.rows // 2), (half + 1) * (self.rows // 2)), total)


def scatter_scratch(rows, columns):
    return [
        pltpu.VMEM((2, SIDE, 2, rows // 4, columns), jnp.bfloat16),
        pltpu.VMEM((2, SIDE, 2, rows // 2, columns), jnp.bfloat16),
        pltpu.VMEM((2, 2, rows // 4, columns), jnp.bfloat16),
        pltpu.VMEM((2, 2, rows // 2, columns), jnp.bfloat16),
    ]


def inverse_rms(values):
    return lax.rsqrt(jnp.mean(values * values, axis=-1, keepdims=True) + EPSILON)


def turn_halves(values):
    return pltpu.roll(values, HEAD_WIDTH // 2, 1)


def head_map(raw, gain, cosine, sine):
    scaled = raw * inverse_rms(raw) * gain
    return scaled * cosine + turn_halves(scaled) * sine


def head_map_back(raw, gain, cosine, sine, grads):
    inverse = inverse_rms(raw)
    unit = raw * inverse
    turned = grads * cosine + turn_halves(grads * sine)
    gain_grads = jnp.sum(turned * unit, axis=0, keepdims=True)
    scaled = turned * gain
    raw_grads = inverse * (scaled - unit * jnp.mean(scaled * unit, axis=-1, keepdims=True))
    return raw_grads, gain_grads


def project_kernel(
    tokens_hbm, shard_hbm, norm_gain_hbm, query_gain_hbm, key_gain_hbm, segments_hbm, waves_hbm,
    q_ref, kv_ref, raw_ref, normed_ref, wkv_ref, wq_ref, rope_ref, bound_ref,
    tokens_ref, norm_gain_ref, query_gain_ref, key_gain_ref, segments_ref, waves_ref,
    send_sems, recv_sems, local_sems,
):
    width = HEAD_WIDTH
    split = QUERY_PER_KEY * width
    torus = Torus(send_sems, recv_sems)
    rows = shard_hbm.shape[0]
    ctx = lax.axis_index("ctx")
    own = pl.ds(pl.multiple_of(ctx * rows, rows), rows)
    moves = (
        (shard_hbm.at[:, split:], wkv_ref.at[own, :]),
        (tokens_hbm, tokens_ref),
        (norm_gain_hbm, norm_gain_ref),
        (shard_hbm.at[:, 0:split], wq_ref.at[own, :]),
        (waves_hbm, waves_ref),
        (segments_hbm, segments_ref),
        (query_gain_hbm, query_gain_ref),
        (key_gain_hbm, key_gain_ref),
    )
    loads = [
        pltpu.make_async_copy(source, target, local_sems.at[i])
        for i, (source, target) in enumerate(moves)
    ]
    for load in loads:
        load.start()
    torus.greet((1, -1))
    loads[0].wait()
    weights_kv = Gather(torus, wkv_ref)
    weights_kv.start()

    count = tokens_ref.shape[0]

    def token_rows(step, part=None, flip=False):
        core = torus.place["core"]
        index = wrap(torus.place["z"] + step) * 2 + (1 - core if flip else core)
        size = count if part is None else count // 2
        start = index * count + (0 if part is None else part * (count // 2))
        return normed_ref.at[pl.ds(pl.multiple_of(start, count // 2), size), :]

    loads[1].wait()
    loads[2].wait()
    tokens = tokens_ref[...].astype(jnp.float32)
    token_rows(0)[...] = (tokens * inverse_rms(tokens) * norm_gain_ref[...]).astype(jnp.bfloat16)
    mine = token_rows(0)
    ring = {step: torus.send(mine, mine, "z", step) for step in (1, -1)}
    pair = {0: torus.send(mine, mine, "core", 1)}

    loads[3].wait()
    weights_q = Gather(torus, wq_ref)
    weights_kv.near()
    weights_q.start()
    for load in loads[4:]:
        load.wait()
    local = rope_ref.shape[1]
    near_cosine, near_sine = waves_ref[0:local, :], waves_ref[local : 2 * local, :]

    def far_wave(i):
        return waves_ref[pl.ds(2 * local + i * SIDE * SIDE + ctx, 1), :]

    rope_ref[0] = far_wave(0) * near_cosine - far_wave(1) * near_sine
    rope_ref[1] = far_wave(3) * near_cosine + far_wave(2) * near_sine
    onward = {}
    for step in (1, -1):
        torus.arrive(ring[step], token_rows(-step))
        piece = token_rows(-step, part_of(step))
        onward[step] = torus.send(piece, piece, "z", step)
        block = token_rows(-step)
        pair[-step] = torus.send(block, block, "core", 1)
    weights_kv.far()
    for step in (1, -1):
        torus.arrive(onward[step], token_rows(2, part_of(step)))
    block = token_rows(2)
    pair[2] = torus.send(block, block, "core", 1)
    weights_kv.cross((0, -1, 1))
    weights_q.near()
    weights_kv.cross((2,))

    segments = segments_ref[...]
    lines = local // segments.shape[1]
    for line in range(lines):
        asked = segments_ref[pl.ds(ctx * lines + line, 1), :]
        first = jnp.zeros(asked.shape, jnp.float32)
        last = jnp.zeros(asked.shape, jnp.float32)
        for number in range(SEGMENTS):
            size = jnp.where(segments == number, 1.0, 0.0)
            size = jnp.sum(jnp.sum(size, axis=0, keepdims=True), axis=1, keepdims=True)
            first = first + jnp.where(asked > number, size, 0.0)
            last = last + jnp.where(asked >= number, size, 0.0)
        columns = slice(line * segments.shape[1], (line + 1) * segments.shape[1])
        bound_ref[0:1, columns] = first
        bound_ref[1:2, columns] = last

    weights_q.far()
    for step in (0, -1, 1, 2):
        torus.arrive(pair[step], token_rows(step, flip=True))
    weights_kv.finish()

    cosine, sine = rope_ref[0], rope_ref[1]
    raw = jnp.dot(normed_ref[...], wkv_ref[...], preferred_element_type=jnp.float32)
    raw_ref[:, split:] = raw[:, :width]
    kv_ref[own, 0:width] = head_map(raw[:, :width], key_gain_ref[...], cosine, sine).astype(
        jnp.bfloat16
    )
    kv_ref[own, width:] = raw[:, width:].astype(jnp.bfloat16)
    weights_q.cross((0, -1, 1))
    keys_values = Gather(torus, kv_ref)
    keys_values.start()
    weights_q.cross((2,))
    keys_values.near()
    weights_q.finish()

    def query_head(g):
        columns = slice(g * width, (g + 1) * width)
        raw = jnp.dot(normed_ref[...], wq_ref[:, columns], preferred_element_type=jnp.float32)
        raw_ref[:, columns] = raw
        q_ref[:, columns] = head_map(raw, query_gain_ref[...], cosine, sine).astype(jnp.bfloat16)

    keys_values.far()
    query_head(0)
    keys_values.cross((0, -1))
    query_head(1)
    keys_values.cross((1, 2))
    query_head(2)
    query_head(3)
    keys_values.finish()
    torus.close()


def project(tokens, shard, norm_gain, query_gain, key_gain, segments, waves):
    rows, columns = shard.shape
    count, depth = tokens.shape
    width = HEAD_WIDTH
    total = segments.shape[0] * segments.shape[1]
    local = total // (SIDE * SIDE)
    split = QUERY_PER_KEY * width
    vmem = pl.BlockSpec(memory_space=pltpu.VMEM)
    hbm = pl.BlockSpec(memory_space=pltpu.HBM)
    copies = 3 * 40 + 8
    bf16, f32 = jnp.bfloat16, jnp.float32
    return pl.pallas_call(
        project_kernel,
        out_shape=(
            jax.ShapeDtypeStruct((local, split), bf16),
            jax.ShapeDtypeStruct((total, 2 * width), bf16),
            jax.ShapeDtypeStruct((local, split + width), f32),
            jax.ShapeDtypeStruct((local, depth), bf16),
            jax.ShapeDtypeStruct((depth, 2 * width), bf16),
            jax.ShapeDtypeStruct((depth, split), bf16),
            jax.ShapeDtypeStruct((2, local, width), f32),
            jax.ShapeDtypeStruct((2, local), f32),
        ),
        in_specs=[hbm] * 7,
        out_specs=(vmem,) * 8,
        scratch_shapes=[
            pltpu.VMEM(tokens.shape, bf16),
            pltpu.VMEM(norm_gain.shape, f32),
            pltpu.VMEM(query_gain.shape, f32),
            pltpu.VMEM(key_gain.shape, f32),
            pltpu.VMEM(segments.shape, jnp.int32),
            pltpu.VMEM(waves.shape, f32),
            pltpu.SemaphoreType.DMA((copies,)),
            pltpu.SemaphoreType.DMA((copies,)),
            pltpu.SemaphoreType.DMA((8,)),
        ],
        compiler_params=pltpu.CompilerParams(
            collective_id=0, has_side_effects=True, vmem_limit_bytes=24 * 1024 * 1024
        ),
        cost_estimate=pl.CostEstimate(
            flops=2 * local * depth * columns, bytes_accessed=2 * depth * columns, transcendentals=0
        ),
    )(tokens, shard, norm_gain, query_gain, key_gain, segments, waves)


def attention_kernel(
    q_ref, kv_ref, up_ref, bound_ref,
    context_ref, dq_ref, dkv_ref,
    exp_ref, q4_ref, q4t_ref, up4_ref, up4t_ref, num_ref, den_ref, corr_ref,
):
    rows = q_ref.shape[0]
    total = kv_ref.shape[0]
    width = HEAD_WIDTH
    block = KEY_BLOCK
    scale = width ** (-0.5)
    start_row = bound_ref[0:1, :]
    end_row = bound_ref[1:2, :]
    low = (jnp.min(start_row) * (1.0 / ALIGN)).astype(jnp.int32) * ALIGN
    high = jnp.max(end_row).astype(jnp.int32)
    steps = lax.div(high - low + (block - 1), block)
    for g in range(QUERY_PER_KEY):
        query = q_ref[:, g * width : (g + 1) * width]
        q4_ref[g] = query
        q4t_ref[g] = query.T
    num_ref[...] = jnp.zeros_like(num_ref)
    den_ref[...] = jnp.zeros_like(den_ref)
    dq_ref[...] = jnp.zeros_like(dq_ref)
    dkv_ref[...] = jnp.zeros_like(dkv_ref)

    def rows_of(i):
        wanted = low + i * block
        first = jnp.minimum(wanted, total - block)
        return wanted, first, pl.ds(pl.multiple_of(first, ALIGN), block)

    def forward(i, carry):
        wanted, first, at = rows_of(i)
        key = kv_ref[at, 0:width]
        value = kv_ref[at, width : 2 * width]
        place = (lax.broadcasted_iota(jnp.int32, (block, rows), 0) + first).astype(jnp.float32)
        floor_row = jnp.maximum(start_row, wanted.astype(jnp.float32))
        mask = (place >= floor_row) & (place < end_row)
        for g in range(QUERY_PER_KEY):
            scores = jnp.dot(key, q4t_ref[g], preferred_element_type=jnp.float32)
            exponent = jnp.where(mask, jnp.exp2(scores * (scale * LOG2E)), 0.0)
            den_ref[g] += jnp.sum(exponent.reshape(block // 8, 8, rows), axis=0)
            rounded = exponent.astype(jnp.bfloat16)
            exp_ref[g, pl.ds(pl.multiple_of(i * block, block), block), :] = rounded
            num_ref[g] += lax.dot_general(
                rounded, value, TN, preferred_element_type=jnp.float32
            )
        return carry

    lax.fori_loop(0, steps, forward, 0)
    for g in range(QUERY_PER_KEY):
        columns = slice(g * width, (g + 1) * width)
        inverse = 1.0 / jnp.sum(den_ref[g].T, axis=1, keepdims=True)
        context = (num_ref[g] * inverse).astype(jnp.bfloat16)
        context_ref[:, columns] = context
        up = (up_ref[:, columns].astype(jnp.float32) * inverse).astype(jnp.bfloat16)
        up4_ref[g] = up
        up4t_ref[g] = up.T
        product = up.astype(jnp.float32) * context.astype(jnp.float32)
        corr_ref[g] = jnp.sum(product.T, axis=0, keepdims=True)

    def backward(i, carry):
        wanted, first, at = rows_of(i)
        key = kv_ref[at, 0:width]
        value = kv_ref[at, width : 2 * width]
        dk = jnp.zeros((block, width), jnp.float32)
        dv = jnp.zeros((block, width), jnp.float32)
        for g in range(QUERY_PER_KEY):
            grads = jnp.dot(value, up4t_ref[g], preferred_element_type=jnp.float32)
            rounded = exp_ref[g, pl.ds(pl.multiple_of(i * block, block), block), :]
            ds = (rounded.astype(jnp.float32) * (grads - corr_ref[g])).astype(jnp.bfloat16)
            dk += jnp.dot(ds, q4_ref[g], preferred_element_type=jnp.float32)
            dv += jnp.dot(rounded, up4_ref[g], preferred_element_type=jnp.float32)
            dq_ref[:, g * width : (g + 1) * width] += lax.dot_general(
                ds, key, TN, preferred_element_type=jnp.float32
            )
        kept = dkv_ref[at, :].astype(jnp.float32)
        dkv_ref[at, 0:width] = (kept[:, 0:width] + dk * scale).astype(jnp.bfloat16)
        dkv_ref[at, width : 2 * width] = (kept[:, width:] + dv).astype(jnp.bfloat16)
        return carry

    lax.fori_loop(0, steps, backward, 0)
    dq_ref[...] = dq_ref[...] * scale


def attention(queries, keys_values, upstream, bounds):
    rows = queries.shape[0]
    total = keys_values.shape[0]
    group = QUERY_PER_KEY
    width = HEAD_WIDTH
    vmem = pl.BlockSpec(memory_space=pltpu.VMEM)
    bf16, f32 = jnp.bfloat16, jnp.float32
    return pl.pallas_call(
        attention_kernel,
        out_shape=(
            jax.ShapeDtypeStruct((rows, group * width), bf16),
            jax.ShapeDtypeStruct((rows, group * width), f32),
            jax.ShapeDtypeStruct((total, 2 * width), bf16),
        ),
        in_specs=[vmem] * 4,
        out_specs=(vmem, vmem, vmem),
        scratch_shapes=[
            pltpu.VMEM((group, total + KEY_BLOCK, rows), bf16),
            pltpu.VMEM((group, rows, width), bf16),
            pltpu.VMEM((group, width, rows), bf16),
            pltpu.VMEM((group, rows, width), bf16),
            pltpu.VMEM((group, width, rows), bf16),
            pltpu.VMEM((group, rows, width), f32),
            pltpu.VMEM((group, 8, rows), f32),
            pltpu.VMEM((group, 1, rows), f32),
        ],
        compiler_params=pltpu.CompilerParams(vmem_limit_bytes=28 * 1024 * 1024),
        cost_estimate=pl.CostEstimate(
            flops=14 * group * rows * total * width,
            bytes_accessed=8 * total * width,
            transcendentals=group * rows * total,
        ),
    )(queries, keys_values, upstream, bounds)


def gradient_kernel(
    dq_ref, dkv_in_ref, raw_ref, normed_ref, wq_ref, wkv_ref, rope_ref, tokens_ref,
    norm_gain_ref, query_gain_ref, key_gain_ref,
    token_grads_ref, projection_grads_ref, gains_ref,
    send_sems, recv_sems, local_sems,
    dkv_ref, jq_ref, jkv_ref, gq_ref, gkv_ref, dkv_sum_ref,
    terms_ref, pair_ref, zfar_ref, znear_ref, gx_ref, gy_ref, gz_ref, gc_ref,
    *boxes,
):
    width = HEAD_WIDTH
    split = QUERY_PER_KEY * width
    torus = Torus(send_sems, recv_sems)
    load = pltpu.make_async_copy(dkv_in_ref, dkv_ref, local_sems.at[0])
    load.start()
    torus.greet((1, 2, 3))
    dkv = Scatter(torus, dkv_ref, *boxes[0:4])
    dwq = Scatter(torus, gq_ref, *boxes[4:8])
    dwkv = Scatter(torus, gkv_ref, *boxes[8:12])
    dkv.start(dkv_in_ref)

    cosine, sine = rope_ref[0], rope_ref[1]
    query_gain_grads = jnp.zeros((1, width), jnp.float32)
    for g in range(QUERY_PER_KEY):
        columns = slice(g * width, (g + 1) * width)
        raw_grads, gain_grads = head_map_back(
            raw_ref[:, columns], query_gain_ref[...], cosine, sine, dq_ref[:, columns]
        )
        jq_ref[:, columns] = raw_grads.astype(jnp.bfloat16)
        query_gain_grads = query_gain_grads + gain_grads
    load.wait()
    dkv.turn()

    def weight_grads(j_ref, g_ref):
        def body(i, carry):
            at = pl.ds(pl.multiple_of(i * 256, 256), 256)
            g_ref[at, :] = lax.dot_general(
                normed_ref[:, at], j_ref[...], TN, preferred_element_type=jnp.float32
            ).astype(jnp.bfloat16)
            return carry

        lax.fori_loop(0, normed_ref.shape[1] // 256, body, 0)

    weight_grads(jq_ref, gq_ref)
    dwq.start()
    dkv.land()
    dkv.turn_two()
    dwq.turn((2, 1))

    def keep_dkv(at, total):
        dkv_sum_ref[at, :] = total

    dkv.finish(keep_dkv)
    raw_grads, key_gain_grads = head_map_back(
        raw_ref[:, split:], key_gain_ref[...], cosine, sine, dkv_sum_ref[:, :width]
    )
    jkv_ref[:, :width] = raw_grads.astype(jnp.bfloat16)
    jkv_ref[:, width:] = dkv_sum_ref[:, width:].astype(jnp.bfloat16)
    weight_grads(jkv_ref, gkv_ref)
    dwkv.start()
    dwq.turn((-1, 0))

    def input_terms(i, carry):
        at = pl.ds(pl.multiple_of(i * 256, 256), 256)
        terms_ref[:, at] = (
            lax.dot_general(jq_ref[...], wq_ref[at, :], NT, preferred_element_type=jnp.float32)
            + lax.dot_general(jkv_ref[...], wkv_ref[at, :], NT, preferred_element_type=jnp.float32)
        ).astype(jnp.bfloat16)
        return carry

    lax.fori_loop(0, terms_ref.shape[1] // 256, input_terms, 0)

    count = tokens_ref.shape[0]

    def term_rows(step, part=None, flip=False):
        core = torus.place["core"]
        index = wrap(torus.place["z"] + step) * 2 + (1 - core if flip else core)
        size = count if part is None else count // 2
        start = index * count + (0 if part is None else part * (count // 2))
        return terms_ref.at[pl.ds(pl.multiple_of(start, count // 2), size), :]

    pair = {
        step: torus.send(term_rows(step, flip=True), pair_ref.at[step % SIDE], "core", 1)
        for step in (2, 1, -1, 0)
    }
    dwq.land((2,))
    dwkv.turn((2,))
    far = {}
    torus.arrive(pair[2], pair_ref.at[2])
    add_to(term_rows(2), pair_ref.at[2])
    for step in (1, -1):
        far[step] = torus.send(
            term_rows(2, part_of(step)), zfar_ref.at[part_of(step)], "z", step
        )
    dwq.land((1, -1))
    dwq.turn_two()
    near = {}
    for step in (1, -1):
        torus.arrive(pair[step], pair_ref.at[step % SIDE])
        add_to(term_rows(step), pair_ref.at[step % SIDE])
        torus.arrive(far[step], zfar_ref.at[part_of(step)])
        add_to(term_rows(step, part_of(step)), zfar_ref.at[part_of(step)])
        near[step] = torus.send(term_rows(step), znear_ref.at[part_of(step)], "z", step)
    dwkv.turn((1, -1, 0))
    dwq.land((0,))
    torus.arrive(pair[0], pair_ref.at[0])
    for step in (1, -1):
        torus.arrive(near[step], znear_ref.at[part_of(step)])
    normed_grads = term_rows(0)[...].astype(jnp.float32) + pair_ref[0].astype(jnp.float32)
    normed_grads = normed_grads + (
        znear_ref[0].astype(jnp.float32) + znear_ref[1].astype(jnp.float32)
    )
    tokens = tokens_ref[...].astype(jnp.float32)
    inverse = inverse_rms(tokens)
    unit = tokens * inverse
    norm_gain_grads = jnp.sum(normed_grads * unit, axis=0, keepdims=True)
    scaled = normed_grads * norm_gain_ref[...]
    token_grads_ref[...] = inverse * (
        scaled - unit * jnp.mean(scaled * unit, axis=-1, keepdims=True)
    )
    lines = tokens.shape[1] // width
    gains_ref[...] = jnp.zeros_like(gains_ref)
    for i in range(lines):
        gains_ref[i : i + 1, :] = norm_gain_grads[:, i * width : (i + 1) * width]
    gains_ref[lines : lines + 1, :] = query_gain_grads
    gains_ref[lines + 1 : lines + 2, :] = key_gain_grads

    def share(axis, box):
        place, size = torus.place[axis], box.shape[0]
        box[place] = gains_ref[...]
        return [
            torus.send(box.at[place], box.at[place], axis, step) for step in range(1, size)
        ]

    def collect(axis, box, sent):
        place, size = torus.place[axis], box.shape[0]
        for step in range(1, size):
            torus.arrive(sent[step - 1], box.at[lax.rem(place + size - step, size)])
        total = box[0]
        for i in range(1, size):
            total = total + box[i]
        gains_ref[...] = total

    def keep_q(at, total):
        projection_grads_ref[at, :split] = total

    def keep_kv(at, total):
        projection_grads_ref[at, split:] = total

    sent = share("z", gz_ref)
    dwkv.land((2, 1))
    collect("z", gz_ref, sent)
    sent = share("core", gc_ref)
    dwkv.land((-1,))
    collect("core", gc_ref, sent)
    sent = share("x", gx_ref)
    dwkv.turn_two()
    dwq.finish(keep_q)
    collect("x", gx_ref, sent)
    sent = share("y", gy_ref)
    dwkv.land((0,))
    dwkv.finish(keep_kv)
    collect("y", gy_ref, sent)
    torus.close()


def gradients(
    dq, dkv, raw, normed, wq, wkv, rope, tokens, norm_gain, query_gain, key_gain
):
    local, depth = normed.shape
    count = tokens.shape[0]
    total = dkv.shape[0]
    width = HEAD_WIDTH
    split = QUERY_PER_KEY * width
    rows = depth // (SIDE * SIDE)
    gains = (depth // width + 8, width)
    vmem = pl.BlockSpec(memory_space=pltpu.VMEM)
    copies = 3 * 40 + 8 + 10
    bf16, f32 = jnp.bfloat16, jnp.float32
    return pl.pallas_call(
        gradient_kernel,
        out_shape=(
            jax.ShapeDtypeStruct((count, depth), f32),
            jax.ShapeDtypeStruct((rows, split + 2 * width), f32),
            jax.ShapeDtypeStruct(gains, f32),
        ),
        in_specs=[vmem] * 11,
        out_specs=(vmem,) * 3,
        scratch_shapes=[
            pltpu.SemaphoreType.DMA((copies,)),
            pltpu.SemaphoreType.DMA((copies,)),
            pltpu.SemaphoreType.DMA((1,)),
            pltpu.VMEM((total, 2 * width), bf16),
            pltpu.VMEM((local, split), bf16),
            pltpu.VMEM((local, 2 * width), bf16),
            pltpu.VMEM((depth, split), bf16),
            pltpu.VMEM((depth, 2 * width), bf16),
            pltpu.VMEM((local, 2 * width), f32),
            pltpu.VMEM((local, depth), bf16),
            pltpu.VMEM((SIDE, count, depth), bf16),
            pltpu.VMEM((2, count // 2, depth), bf16),
            pltpu.VMEM((2, count, depth), bf16),
            pltpu.VMEM((SIDE,) + gains, f32),
            pltpu.VMEM((SIDE,) + gains, f32),
            pltpu.VMEM((SIDE,) + gains, f32),
            pltpu.VMEM((2,) + gains, f32),
        ]
        + scatter_scratch(total // (SIDE * SIDE), 2 * width)
        + scatter_scratch(rows, split)
        + scatter_scratch(rows, 2 * width),
        compiler_params=pltpu.CompilerParams(
            collective_id=1, has_side_effects=True, vmem_limit_bytes=40 * 1024 * 1024
        ),
        cost_estimate=pl.CostEstimate(
            flops=4 * local * depth * (split + 2 * width),
            bytes_accessed=4 * depth * (split + 2 * width),
            transcendentals=0,
        ),
    )(dq, dkv, raw, normed, wq, wkv, rope, tokens, norm_gain, query_gain, key_gain)


def finish_kernel(
    token_ref, projection_ref, gains_ref,
    token_out, projection_out, norm_out, query_out, key_out,
    sems,
):
    copies = [
        pltpu.make_async_copy(token_ref, token_out, sems.at[0]),
        pltpu.make_async_copy(projection_ref, projection_out, sems.at[1]),
    ]
    for copy in copies:
        copy.start()
    lines = norm_out.shape[0]
    norm_out[...] = gains_ref[0:lines, :]
    query_out[...] = gains_ref[lines : lines + 1, :]
    key_out[...] = gains_ref[lines + 1 : lines + 2, :]
    for copy in copies:
        copy.wait()


def finish(token_grads, projection_grads, gains):
    width = HEAD_WIDTH
    vmem = pl.BlockSpec(memory_space=pltpu.VMEM)
    hbm = pl.BlockSpec(memory_space=pltpu.HBM)
    anywhere = pl.BlockSpec(memory_space=pl.ANY)
    f32 = jnp.float32
    return pl.pallas_call(
        finish_kernel,
        out_shape=(
            jax.ShapeDtypeStruct(token_grads.shape, f32),
            jax.ShapeDtypeStruct(projection_grads.shape, f32),
            jax.ShapeDtypeStruct((token_grads.shape[1] // width, width), f32),
            jax.ShapeDtypeStruct((1, width), f32),
            jax.ShapeDtypeStruct((1, width), f32),
        ),
        in_specs=[anywhere, anywhere, vmem],
        out_specs=(hbm, hbm, vmem, vmem, vmem),
        scratch_shapes=[pltpu.SemaphoreType.DMA((2,))],
        compiler_params=pltpu.CompilerParams(vmem_limit_bytes=4 * 1024 * 1024),
    )(token_grads, projection_grads, gains)


def rope_waves(local, blocks, width):
    half = width // 2
    frequency = THETA ** (-2.0 * np.arange(half) / width)
    frequency = np.concatenate([frequency, frequency])
    sign = np.concatenate([-np.ones(half), np.ones(half)])
    near = np.arange(local)[:, None] * frequency[None, :]
    far = np.arange(blocks)[:, None] * float(local) * frequency[None, :]
    waves = [np.cos(near), np.sin(near), np.cos(far), np.sin(far), sign * np.cos(far), sign * np.sin(far)]
    return np.concatenate(waves, axis=0).astype(np.float32)


def on_device(tokens, projection, norm_gain, query_gain, key_gain, segment_ids, context_cotangent):
    local = context_cotangent.shape[0]
    waves = jnp.asarray(rope_waves(local, SIDE * SIDE, HEAD_WIDTH))
    norm_gain = norm_gain.reshape(1, -1)
    query_gain = query_gain.reshape(1, -1)
    key_gain = key_gain.reshape(1, -1)
    segments = segment_ids.reshape(-1, 128)
    queries, keys_values, raw, normed, wkv, wq, rope, bounds = project(
        tokens, projection, norm_gain, query_gain, key_gain, segments, waves
    )
    context, query_grads, kv_grads = attention(queries, keys_values, context_cotangent, bounds)
    token_grads, projection_grads, gains = gradients(
        query_grads, kv_grads, raw, normed, wq, wkv, rope, tokens, norm_gain, query_gain, key_gain
    )
    token_grads, projection_grads, norm_gains, query_gains, key_gains = finish(
        token_grads, projection_grads, gains
    )
    return (
        context,
        token_grads,
        projection_grads,
        norm_gains.reshape(-1),
        query_gains.reshape(-1),
        key_gains.reshape(-1),
    )


def solution(mesh):
    placed = (
        P(("dp", "ctx", "tp"), None),
        P("ctx", "tp"),
        P(),
        P(),
        P(),
        P("dp"),
        P(("dp", "ctx"), "tp"),
    )
    return jax.shard_map(
        on_device,
        mesh=mesh,
        in_specs=placed,
        out_specs=(
            P(("dp", "ctx"), "tp"),
            P(("dp", "ctx", "tp"), None),
            P(("dp", "ctx"), "tp"),
            P("dp"),
            P("dp"),
            P("dp"),
        ),
        check_vma=False,
    )
```

```python
import jax
import jax.numpy as jnp
import numpy as np
from jax import lax
from jax.experimental import pallas as pl
from jax.experimental.pallas import tpu as pltpu
from jax.sharding import PartitionSpec as P

HEAD_WIDTH = 128
QUERY_PER_KEY = 4
SEGMENTS = 16
SIDE = 4
EPSILON = 1e-06
THETA = 1000000.0
LOG2E = 1.4426950408889634
MESH = pl.DeviceIdType.MESH
NT = (((1,), (1,)), ((), ()))
TN = (((0,), (0,)), ((), ()))


def wrap(value):
    return lax.rem(value + 2 * SIDE, SIDE)


def part_of(step):
    return 0 if step == 1 else 1


class Torus:
    def __init__(self, send_sems, recv_sems):
        ctx, tp = lax.axis_index("ctx"), lax.axis_index("tp")
        self.place = {
            "y": lax.div(ctx, SIDE),
            "x": lax.rem(ctx, SIDE),
            "z": lax.div(tp, 2),
            "core": lax.rem(tp, 2),
        }
        self.tp = tp
        self.sems = (send_sems, recv_sems)
        self.sent = []

    def along(self, axis, step):
        at = self.place
        if axis == "x":
            return {"ctx": at["y"] * SIDE + wrap(at["x"] + step)}
        if axis == "y":
            return {"ctx": wrap(at["y"] + step) * SIDE + at["x"]}
        if axis == "z":
            return {"tp": wrap(at["z"] + step) * 2 + at["core"]}
        return {"tp": at["z"] * 2 + 1 - at["core"]}

    def greet(self, steps):
        barrier = pltpu.get_barrier_semaphore()
        partners = [(axis, step) for axis in ("x", "y", "z") for step in steps] + [("core", 1)]
        for axis, step in partners:
            pl.semaphore_signal(
                barrier, inc=1, device_id=self.along(axis, step), device_id_type=MESH
            )
        pl.semaphore_wait(barrier, len(partners))

    def copy(self, index, source, target, axis, step):
        return pltpu.make_async_remote_copy(
            src_ref=source,
            dst_ref=target,
            send_sem=self.sems[0].at[index],
            recv_sem=self.sems[1].at[index],
            device_id=self.along(axis, step),
            device_id_type=MESH,
        )

    def send(self, source, target, axis, step):
        index = len(self.sent)
        copy = self.copy(index, source, target, axis, step)
        copy.start()
        self.sent.append(copy)
        return index

    def arrive(self, index, target):
        self.copy(index, target, target, "core", 1).wait_recv()

    def close(self):
        for copy in self.sent:
            copy.wait_send()


class Blocks:
    def __init__(self, torus, data, orders):
        self.torus, self.data, self.orders = torus, data, orders
        self.rows = data.shape[0] // (SIDE * SIDE)
        self.keys = {}

    def at(self, half, first, second, part=None):
        offset = dict(zip(self.orders[half], (first, second)))
        place = self.torus.place
        block = wrap(place["y"] + offset["y"]) * SIDE + wrap(place["x"] + offset["x"])
        rows = self.rows
        start = block * rows + half * (rows // 2)
        if part is not None:
            start = start + part * (rows // 4)
        size = rows // 2 if part is None else rows // 4
        return self.data.at[pl.ds(pl.multiple_of(start, rows // 4), size), :]

    def send(self, key, source, target, axis, step):
        self.keys[key] = self.torus.send(source, target, axis, step)

    def arrive(self, key, target):
        self.torus.arrive(self.keys[key], target)


class Gather(Blocks):
    def __init__(self, torus, data):
        super().__init__(torus, data, (("x", "y"), ("y", "x")))

    def pass_on(self, half, first):
        for step in (1, -1):
            block = self.at(half, first, 0)
            self.send(("q", half, first, step), block, block, self.orders[half][1], step)

    def start(self):
        for half in (0, 1):
            for step in (1, -1):
                block = self.at(half, 0, 0)
                self.send(("p", half, step), block, block, self.orders[half][0], step)
        for half in (0, 1):
            self.pass_on(half, 0)

    def near(self):
        for half in (0, 1):
            for step in (1, -1):
                self.arrive(("p", half, step), self.at(half, -step, 0))
                block = self.at(half, -step, 0, part_of(step))
                self.send(("f", half, step), block, block, self.orders[half][0], step)
        for half in (0, 1):
            for step in (1, -1):
                self.pass_on(half, -step)

    def far(self):
        for half in (0, 1):
            for step in (1, -1):
                self.arrive(("f", half, step), self.at(half, 2, 0, part_of(step)))
            self.pass_on(half, 2)

    def cross(self, firsts):
        for first in firsts:
            for half in (0, 1):
                for step in (1, -1):
                    self.arrive(("q", half, first, step), self.at(half, first, -step))
                    block = self.at(half, first, -step, part_of(step))
                    self.send(("g", half, first, step), block, block, self.orders[half][1], step)

    def finish(self):
        for first in (0, -1, 1, 2):
            for half in (0, 1):
                for step in (1, -1):
                    self.arrive(("g", half, first, step), self.at(half, first, 2, part_of(step)))


def add_to(target, *sources):
    total = target[...].astype(jnp.float32)
    for source in sources:
        total = total + source[...].astype(jnp.float32)
    target[...] = total.astype(target.dtype)


class Scatter(Blocks):
    def __init__(self, torus, data, far_one, near_one, far_two, near_two):
        super().__init__(torus, data, (("y", "x"), ("x", "y")))
        self.far_one, self.near_one = far_one, near_one
        self.far_two, self.near_two = far_two, near_two

    def start(self, halves=(0, 1)):
        for second in (2, 1, -1, 0):
            for half in halves:
                for step in (1, -1):
                    self.send(
                        ("f1", half, second, step),
                        self.at(half, 2, second, part_of(step)),
                        self.far_one.at[half, second % SIDE, part_of(step)],
                        self.orders[half][0],
                        step,
                    )

    def turn(self, seconds=(2, 1, -1, 0), steps=(1, -1)):
        for second in seconds:
            for half in (0, 1):
                for step in steps:
                    landed = self.far_one.at[half, second % SIDE, part_of(step)]
                    self.arrive(("f1", half, second, step), landed)
                    add_to(self.at(half, step, second, part_of(step)), landed)
                    self.send(
                        ("n1", half, second, step),
                        self.at(half, step, second),
                        self.near_one.at[half, second % SIDE, part_of(step)],
                        self.orders[half][0],
                        step,
                    )

    def land(self, seconds=(2, 1, -1, 0)):
        for second in seconds:
            for half in (0, 1):
                landed = [self.near_one.at[half, second % SIDE, part] for part in (0, 1)]
                for step in (1, -1):
                    self.arrive(("n1", half, second, step), landed[part_of(step)])
                add_to(self.at(half, 0, second), *landed)
                if second == 2:
                    for step in (1, -1):
                        self.send(
                            ("f2", half, step),
                            self.at(half, 0, 2, part_of(step)),
                            self.far_two.at[half, part_of(step)],
                            self.orders[half][1],
                            step,
                        )

    def turn_two(self):
        for half in (0, 1):
            for step in (1, -1):
                landed = self.far_two.at[half, part_of(step)]
                self.arrive(("f2", half, step), landed)
                add_to(self.at(half, 0, step, part_of(step)), landed)
                self.send(
                    ("n2", half, step),
                    self.at(half, 0, step),
                    self.near_two.at[half, part_of(step)],
                    self.orders[half][1],
                    step,
                )

    def finish(self, store):
        for half in (0, 1):
            landed = [self.near_two.at[half, part] for part in (0, 1)]
            for step in (1, -1):
                self.arrive(("n2", half, step), landed[part_of(step)])
            total = self.at(half, 0, 0)[...].astype(jnp.float32)
            for source in landed:
                total = total + source[...].astype(jnp.float32)
            store(slice(half * (self.rows // 2), (half + 1) * (self.rows // 2)), total)


def scatter_scratch(rows, columns):
    return [
        pltpu.VMEM((2, SIDE, 2, rows // 4, columns), jnp.bfloat16),
        pltpu.VMEM((2, SIDE, 2, rows // 2, columns), jnp.bfloat16),
        pltpu.VMEM((2, 2, rows // 4, columns), jnp.bfloat16),
        pltpu.VMEM((2, 2, rows // 2, columns), jnp.bfloat16),
    ]


def inverse_rms(values):
    return lax.rsqrt(jnp.mean(values * values, axis=-1, keepdims=True) + EPSILON)


def turn_halves(values):
    return pltpu.roll(values, HEAD_WIDTH // 2, 1)


def head_map(raw, gain, cosine, sine):
    scaled = raw * inverse_rms(raw) * gain
    return scaled * cosine + turn_halves(scaled) * sine


def head_map_back(raw, gain, cosine, sine, grads):
    inverse = inverse_rms(raw)
    unit = raw * inverse
    turned = grads * cosine + turn_halves(grads * sine)
    gain_grads = jnp.sum(turned * unit, axis=0, keepdims=True)
    scaled = turned * gain
    raw_grads = inverse * (scaled - unit * jnp.mean(scaled * unit, axis=-1, keepdims=True))
    return raw_grads, gain_grads


def layer_kernel(
    tokens_hbm, shard_hbm, norm_gain_hbm, query_gain_hbm, key_gain_hbm, segments_hbm, waves_hbm, up_hbm,
    context_ref, token_grads_ref, projection_grads_ref, gains_ref,
    send_sems, recv_sems, local_sems,
    tokens_ref, norm_gain_ref, query_gain_ref, key_gain_ref, segments_ref, waves_ref, up_ref,
    kv_ref, raw_ref, normed_ref, wkv_ref, wqa_ref, wqb_ref, rope_ref, bound_ref,
    exp_ref, q4_ref, q4t_ref, up4_ref, up4t_ref, num_ref, den_ref, corr_ref, dq_ref,
    dkv_ref, jq_ref, jkv_ref, gq_ref, gkv_ref, dkv_sum_ref,
    terms_ref, pair_ref, zfar_ref, znear_ref, gx_ref, gy_ref, gz_ref, gc_ref,
    *boxes,
):
    width = HEAD_WIDTH
    split = QUERY_PER_KEY * width
    pair_width = 2 * width
    torus = Torus(send_sems, recv_sems)
    rows = shard_hbm.shape[0]
    ctx = lax.axis_index("ctx")
    own = pl.ds(pl.multiple_of(ctx * rows, rows), rows)
    moves = (
        (shard_hbm.at[:, 0:pair_width], wqa_ref.at[own, :]),
        (tokens_hbm, tokens_ref),
        (norm_gain_hbm, norm_gain_ref),
        (shard_hbm.at[:, split:], wkv_ref.at[own, :]),
        (shard_hbm.at[:, pair_width:split], wqb_ref.at[own, :]),
        (waves_hbm, waves_ref),
        (segments_hbm, segments_ref),
        (query_gain_hbm, query_gain_ref),
        (key_gain_hbm, key_gain_ref),
        (up_hbm, up_ref),
    )
    loads = [
        pltpu.make_async_copy(source, target, local_sems.at[i])
        for i, (source, target) in enumerate(moves)
    ]
    for load in loads:
        load.start()
    torus.greet((1, 2, 3))
    loads[0].wait()
    weights_qa = Gather(torus, wqa_ref)
    weights_kv = Gather(torus, wkv_ref)
    weights_qb = Gather(torus, wqb_ref)
    keys_values = Gather(torus, kv_ref)
    weights_qa.start()

    count = tokens_ref.shape[0]

    def token_rows(step, part=None, flip=False):
        core = torus.place["core"]
        index = wrap(torus.place["z"] + step) * 2 + (1 - core if flip else core)
        size = count if part is None else count // 2
        start = index * count + (0 if part is None else part * (count // 2))
        return normed_ref.at[pl.ds(pl.multiple_of(start, count // 2), size), :]

    loads[1].wait()
    loads[2].wait()
    tokens = tokens_ref[...].astype(jnp.float32)
    token_rows(0)[...] = (tokens * inverse_rms(tokens) * norm_gain_ref[...]).astype(jnp.bfloat16)
    mine = token_rows(0)
    ring = {step: torus.send(mine, mine, "z", step) for step in (1, -1)}
    pair = {0: torus.send(mine, mine, "core", 1)}

    loads[3].wait()
    weights_qa.near()
    weights_kv.start()
    for load in loads[4:]:
        load.wait()
    local = rope_ref.shape[1]
    near_cosine, near_sine = waves_ref[0:local, :], waves_ref[local : 2 * local, :]

    def far_wave(i):
        return waves_ref[pl.ds(2 * local + i * SIDE * SIDE + ctx, 1), :]

    rope_ref[0] = far_wave(0) * near_cosine - far_wave(1) * near_sine
    rope_ref[1] = far_wave(3) * near_cosine + far_wave(2) * near_sine
    onward = {}
    for step in (1, -1):
        torus.arrive(ring[step], token_rows(-step))
        piece = token_rows(-step, part_of(step))
        onward[step] = torus.send(piece, piece, "z", step)
        block = token_rows(-step)
        pair[-step] = torus.send(block, block, "core", 1)
    weights_qa.far()
    for step in (1, -1):
        torus.arrive(onward[step], token_rows(2, part_of(step)))
    block = token_rows(2)
    pair[2] = torus.send(block, block, "core", 1)
    weights_qa.cross((0, -1, 1))
    weights_kv.near()
    weights_qa.cross((2,))
    weights_qb.start()

    segments = segments_ref[...]
    lines = local // segments.shape[1]
    for line in range(lines):
        asked = segments_ref[pl.ds(ctx * lines + line, 1), :]
        first = jnp.zeros(asked.shape, jnp.float32)
        last = jnp.zeros(asked.shape, jnp.float32)
        for number in range(SEGMENTS):
            size = jnp.where(segments == number, 1.0, 0.0)
            size = jnp.sum(jnp.sum(size, axis=0, keepdims=True), axis=1, keepdims=True)
            first = first + jnp.where(asked > number, size, 0.0)
            last = last + jnp.where(asked >= number, size, 0.0)
        columns = slice(line * segments.shape[1], (line + 1) * segments.shape[1])
        bound_ref[0:1, columns] = first
        bound_ref[1:2, columns] = last

    weights_kv.far()
    for step in (0, -1, 1, 2):
        torus.arrive(pair[step], token_rows(step, flip=True))
    weights_qa.finish()
    cosine, sine = rope_ref[0], rope_ref[1]

    def query_heads(weights_ref, heads):
        both = jnp.dot(normed_ref[...], weights_ref[...], preferred_element_type=jnp.float32)
        for i, g in enumerate(heads):
            raw = both[:, i * width : (i + 1) * width]
            raw_ref[:, g * width : (g + 1) * width] = raw
            query = head_map(raw, query_gain_ref[...], cosine, sine).astype(jnp.bfloat16)
            q4_ref[g] = query
            q4t_ref[g] = query.T

    weights_kv.cross((0, -1))
    query_heads(wqa_ref, (0, 1))
    weights_kv.cross((1,))
    weights_qb.near()
    weights_kv.cross((2,))
    weights_qb.far()
    weights_kv.finish()
    raw = jnp.dot(normed_ref[...], wkv_ref[...], preferred_element_type=jnp.float32)
    raw_ref[:, split:] = raw[:, :width]
    kv_ref[own, 0:width] = head_map(raw[:, :width], key_gain_ref[...], cosine, sine).astype(
        jnp.bfloat16
    )
    kv_ref[own, width:] = raw[:, width:].astype(jnp.bfloat16)
    weights_qb.cross((0, -1, 1))
    keys_values.start()
    weights_qb.cross((2,))
    keys_values.near()
    weights_qb.finish()
    scale = width ** (-0.5)
    half_rows = local // 2
    start_row, end_row = bound_ref[0:1, :], bound_ref[1:2, :]
    num_ref[...] = jnp.zeros_like(num_ref)
    den_ref[...] = jnp.zeros_like(den_ref)
    dq_ref[...] = jnp.zeros_like(dq_ref)

    def pieces(half, offset):
        across = wrap(torus.place["y"] + offset) * SIDE * (1 - half)
        base = across + wrap(torus.place["x"] + offset) * half
        stride = 1 + (SIDE - 1) * half
        return [
            pl.multiple_of((base + i * stride) * local + half * half_rows, half_rows)
            for i in range(SIDE)
        ]

    def both_halves(step, offset):
        def body(half, carry):
            step(half, offset)
            return carry

        lax.fori_loop(0, 2, body, 0)

    def key_rows(starts):
        parts = [kv_ref[pl.ds(start, half_rows), :] for start in starts]
        both = jnp.concatenate(parts, axis=0)
        return both[:, 0:width], both[:, width:]

    def slot_of(half, offset):
        return half * SIDE + offset % SIDE

    def forward(half, offset):
        starts = pieces(half, offset)
        key, value = key_rows(starts)
        line = lax.broadcasted_iota(jnp.int32, (half_rows, local), 0)
        place = jnp.concatenate([line + start for start in starts], axis=0).astype(jnp.float32)
        mask = (place >= start_row) & (place < end_row)
        for g in range(QUERY_PER_KEY):
            scores = jnp.dot(key, q4t_ref[g], preferred_element_type=jnp.float32)
            exponent = jnp.where(mask, jnp.exp2(scores * (scale * LOG2E)), 0.0)
            den_ref[g] += jnp.sum(exponent.reshape(SIDE * half_rows // 8, 8, local), axis=0)
            rounded = exponent.astype(jnp.bfloat16)
            exp_ref[slot_of(half, offset), g] = rounded
            num_ref[g] += lax.dot_general(rounded, value, TN, preferred_element_type=jnp.float32)

    def backward(half, offset):
        starts = pieces(half, offset)
        key, value = key_rows(starts)
        dk = jnp.zeros((SIDE * half_rows, width), jnp.float32)
        dv = jnp.zeros((SIDE * half_rows, width), jnp.float32)
        for g in range(QUERY_PER_KEY):
            grads = jnp.dot(value, up4t_ref[g], preferred_element_type=jnp.float32)
            rounded = exp_ref[slot_of(half, offset), g]
            ds = (rounded.astype(jnp.float32) * (grads - corr_ref[g])).astype(jnp.bfloat16)
            dk += jnp.dot(ds, q4_ref[g], preferred_element_type=jnp.float32)
            dv += jnp.dot(rounded, up4_ref[g], preferred_element_type=jnp.float32)
            dq_ref[:, g * width : (g + 1) * width] += lax.dot_general(
                ds, key, TN, preferred_element_type=jnp.float32
            )
        for i, start in enumerate(starts):
            rows_here = slice(i * half_rows, (i + 1) * half_rows)
            at = pl.ds(start, half_rows)
            dkv_ref[at, 0:width] = (dk[rows_here] * scale).astype(jnp.bfloat16)
            dkv_ref[at, width:] = dv[rows_here].astype(jnp.bfloat16)

    keys_values.far()
    query_heads(wqb_ref, (2, 3))
    keys_values.cross((0, -1))
    both_halves(forward, 0)
    keys_values.cross((1, 2))
    both_halves(forward, -1)
    both_halves(forward, 1)
    keys_values.finish()
    both_halves(forward, 2)

    for g in range(QUERY_PER_KEY):
        columns = slice(g * width, (g + 1) * width)
        inverse = 1.0 / jnp.sum(den_ref[g].T, axis=1, keepdims=True)
        context = (num_ref[g] * inverse).astype(jnp.bfloat16)
        context_ref[:, columns] = context
        up = (up_ref[:, columns].astype(jnp.float32) * inverse).astype(jnp.bfloat16)
        up4_ref[g] = up
        up4t_ref[g] = up.T
        product = up.astype(jnp.float32) * context.astype(jnp.float32)
        corr_ref[g] = jnp.sum(product.T, axis=0, keepdims=True)

    dkv = Scatter(torus, dkv_ref, *boxes[0:4])
    dwq = Scatter(torus, gq_ref, *boxes[4:8])
    dwkv = Scatter(torus, gkv_ref, *boxes[8:12])
    both_halves(backward, 2)
    dkv.start()
    for offset in (1, -1):
        both_halves(backward, offset)
        dkv.turn(steps=(offset,))
    both_halves(backward, 0)
    dkv.land()

    query_gain_grads = jnp.zeros((1, width), jnp.float32)
    for g in range(QUERY_PER_KEY):
        columns = slice(g * width, (g + 1) * width)
        raw_grads, gain_grads = head_map_back(
            raw_ref[:, columns], query_gain_ref[...], cosine, sine, dq_ref[:, columns] * scale
        )
        jq_ref[:, columns] = raw_grads.astype(jnp.bfloat16)
        query_gain_grads = query_gain_grads + gain_grads

    def weight_grads(j_ref, g_ref):
        def piece(half, offset):
            starts = pieces(half, offset)
            rows = jnp.concatenate(
                [normed_ref[:, pl.ds(start, half_rows)] for start in starts], axis=1
            )
            grads = lax.dot_general(rows, j_ref[...], TN, preferred_element_type=jnp.float32)
            for i, start in enumerate(starts):
                g_ref[pl.ds(start, half_rows), :] = grads[
                    i * half_rows : (i + 1) * half_rows
                ].astype(jnp.bfloat16)

        return piece

    query_weights = weight_grads(jq_ref, gq_ref)
    both_halves(query_weights, 2)
    dwq.start()
    dkv.turn_two()
    for offset in (1, -1, 0):
        both_halves(query_weights, offset)

    def keep_dkv(at, total):
        dkv_sum_ref[at, :] = total

    dkv.finish(keep_dkv)
    raw_grads, key_gain_grads = head_map_back(
        raw_ref[:, split:], key_gain_ref[...], cosine, sine, dkv_sum_ref[:, :width]
    )
    jkv_ref[:, :width] = raw_grads.astype(jnp.bfloat16)
    jkv_ref[:, width:] = dkv_sum_ref[:, width:].astype(jnp.bfloat16)
    pair_weights = weight_grads(jkv_ref, gkv_ref)
    both_halves(pair_weights, 2)
    dwkv.start()
    dwq.turn()
    for offset in (1, -1, 0):
        both_halves(pair_weights, offset)

    def input_terms(i, carry):
        at = pl.ds(pl.multiple_of(i * 256, 256), 256)
        terms_ref[:, at] = (
            lax.dot_general(
                jq_ref[:, 0:pair_width], wqa_ref[at, :], NT, preferred_element_type=jnp.float32
            )
            + lax.dot_general(
                jq_ref[:, pair_width:], wqb_ref[at, :], NT, preferred_element_type=jnp.float32
            )
            + lax.dot_general(jkv_ref[...], wkv_ref[at, :], NT, preferred_element_type=jnp.float32)
        ).astype(jnp.bfloat16)
        return carry

    lax.fori_loop(0, terms_ref.shape[1] // 256, input_terms, 0)

    def term_rows(step, part=None, flip=False):
        core = torus.place["core"]
        index = wrap(torus.place["z"] + step) * 2 + (1 - core if flip else core)
        size = count if part is None else count // 2
        start = index * count + (0 if part is None else part * (count // 2))
        return terms_ref.at[pl.ds(pl.multiple_of(start, count // 2), size), :]

    pair = {
        step: torus.send(term_rows(step, flip=True), pair_ref.at[step % SIDE], "core", 1)
        for step in (2, 1, -1, 0)
    }
    torus.arrive(pair[2], pair_ref.at[2])
    add_to(term_rows(2), pair_ref.at[2])
    far = {}
    for step in (1, -1):
        far[step] = torus.send(
            term_rows(2, part_of(step)), zfar_ref.at[part_of(step)], "z", step
        )
    dwkv.turn()
    near = {}
    for step in (1, -1):
        torus.arrive(pair[step], pair_ref.at[step % SIDE])
        add_to(term_rows(step), pair_ref.at[step % SIDE])
        torus.arrive(far[step], zfar_ref.at[part_of(step)])
        add_to(term_rows(step, part_of(step)), zfar_ref.at[part_of(step)])
        near[step] = torus.send(term_rows(step), znear_ref.at[part_of(step)], "z", step)
    dwq.land((2, 1, -1))
    dwq.turn_two()
    torus.arrive(pair[0], pair_ref.at[0])
    for step in (1, -1):
        torus.arrive(near[step], znear_ref.at[part_of(step)])
    normed_grads = term_rows(0)[...].astype(jnp.float32) + pair_ref[0].astype(jnp.float32)
    normed_grads = normed_grads + (
        znear_ref[0].astype(jnp.float32) + znear_ref[1].astype(jnp.float32)
    )
    tokens = tokens_ref[...].astype(jnp.float32)
    inverse = inverse_rms(tokens)
    unit = tokens * inverse
    norm_gain_grads = jnp.sum(normed_grads * unit, axis=0, keepdims=True)
    scaled = normed_grads * norm_gain_ref[...]
    token_grads_ref[...] = inverse * (
        scaled - unit * jnp.mean(scaled * unit, axis=-1, keepdims=True)
    )
    lines = tokens.shape[1] // width
    gains_ref[...] = jnp.zeros_like(gains_ref)
    for i in range(lines):
        gains_ref[i : i + 1, :] = norm_gain_grads[:, i * width : (i + 1) * width]
    gains_ref[lines : lines + 1, :] = query_gain_grads
    gains_ref[lines + 1 : lines + 2, :] = key_gain_grads

    def share(axis, box):
        place, size = torus.place[axis], box.shape[0]
        box[place] = gains_ref[...]
        return [
            torus.send(box.at[place], box.at[place], axis, step) for step in range(1, size)
        ]

    def collect(axis, box, sent):
        place, size = torus.place[axis], box.shape[0]
        for step in range(1, size):
            torus.arrive(sent[step - 1], box.at[lax.rem(place + size - step, size)])
        total = box[0]
        for i in range(1, size):
            total = total + box[i]
        gains_ref[...] = total

    def keep_q(at, total):
        projection_grads_ref[at, :split] = total

    def keep_kv(at, total):
        projection_grads_ref[at, split:] = total

    sent = share("z", gz_ref)
    dwq.land((0,))
    collect("z", gz_ref, sent)
    sent = share("core", gc_ref)
    dwkv.land((2, 1))
    collect("core", gc_ref, sent)
    sent = share("x", gx_ref)
    dwkv.land((-1,))
    dwkv.turn_two()
    collect("x", gx_ref, sent)
    sent = share("y", gy_ref)
    dwkv.land((0,))
    dwq.finish(keep_q)
    collect("y", gy_ref, sent)
    dwkv.finish(keep_kv)
    torus.close()


def layer(tokens, shard, norm_gain, query_gain, key_gain, segments, waves, upstream):
    rows, columns = shard.shape
    count, depth = tokens.shape
    local = upstream.shape[0]
    total = local * SIDE * SIDE
    group, width = QUERY_PER_KEY, HEAD_WIDTH
    split = group * width
    gains = (depth // width + 8, width)
    copies = 7 * 40 + 8 + 8 + 10
    bf16, f32 = jnp.bfloat16, jnp.float32
    vmem = pl.BlockSpec(memory_space=pltpu.VMEM)
    hbm = pl.BlockSpec(memory_space=pltpu.HBM)
    return pl.pallas_call(
        layer_kernel,
        out_shape=(
            jax.ShapeDtypeStruct((local, split), bf16),
            jax.ShapeDtypeStruct((count, depth), f32),
            jax.ShapeDtypeStruct((rows, columns), f32),
            jax.ShapeDtypeStruct(gains, f32),
        ),
        in_specs=[hbm] * 8,
        out_specs=(vmem,) * 4,
        scratch_shapes=[
            pltpu.SemaphoreType.DMA((copies,)),
            pltpu.SemaphoreType.DMA((copies,)),
            pltpu.SemaphoreType.DMA((10,)),
            pltpu.VMEM(tokens.shape, bf16),
            pltpu.VMEM(norm_gain.shape, f32),
            pltpu.VMEM(query_gain.shape, f32),
            pltpu.VMEM(key_gain.shape, f32),
            pltpu.VMEM(segments.shape, jnp.int32),
            pltpu.VMEM(waves.shape, f32),
            pltpu.VMEM(upstream.shape, bf16),
            pltpu.VMEM((total, 2 * width), bf16),
            pltpu.VMEM((local, split + width), f32),
            pltpu.VMEM((local, depth), bf16),
            pltpu.VMEM((depth, 2 * width), bf16),
            pltpu.VMEM((depth, split // 2), bf16),
            pltpu.VMEM((depth, split // 2), bf16),
            pltpu.VMEM((2, local, width), f32),
            pltpu.VMEM((2, local), f32),
            pltpu.VMEM((2 * SIDE, group, total // (2 * SIDE), local), bf16),
            pltpu.VMEM((group, local, width), bf16),
            pltpu.VMEM((group, width, local), bf16),
            pltpu.VMEM((group, local, width), bf16),
            pltpu.VMEM((group, width, local), bf16),
            pltpu.VMEM((group, local, width), f32),
            pltpu.VMEM((group, 8, local), f32),
            pltpu.VMEM((group, 1, local), f32),
            pltpu.VMEM((local, split), f32),
            pltpu.VMEM((total, 2 * width), bf16),
            pltpu.VMEM((local, split), bf16),
            pltpu.VMEM((local, 2 * width), bf16),
            pltpu.VMEM((depth, split), bf16),
            pltpu.VMEM((depth, 2 * width), bf16),
            pltpu.VMEM((local, 2 * width), f32),
            pltpu.VMEM((local, depth), bf16),
            pltpu.VMEM((SIDE, count, depth), bf16),
            pltpu.VMEM((2, count // 2, depth), bf16),
            pltpu.VMEM((2, count, depth), bf16),
            pltpu.VMEM((SIDE,) + gains, f32),
            pltpu.VMEM((SIDE,) + gains, f32),
            pltpu.VMEM((SIDE,) + gains, f32),
            pltpu.VMEM((2,) + gains, f32),
        ]
        + scatter_scratch(local, 2 * width)
        + scatter_scratch(rows, split)
        + scatter_scratch(rows, 2 * width),
        compiler_params=pltpu.CompilerParams(
            collective_id=0, has_side_effects=True, vmem_limit_bytes=60 * 1024 * 1024
        ),
        cost_estimate=pl.CostEstimate(
            flops=6 * local * depth * columns + 14 * group * local * total * width,
            bytes_accessed=8 * depth * columns,
            transcendentals=group * local * total,
        ),
    )(tokens, shard, norm_gain, query_gain, key_gain, segments, waves, upstream)


def finish_kernel(
    context_ref, token_ref, projection_ref, gains_ref,
    context_out, token_out, projection_out, norm_out, query_out, key_out,
    context_box, token_box, projection_box, gains_box, sems,
):
    loads, stores = [], []
    for i, (source, box, target) in enumerate(
        (
            (gains_ref, gains_box, None),
            (projection_ref, projection_box, projection_out),
            (token_ref, token_box, token_out),
            (context_ref, context_box, context_out),
        )
    ):
        loads.append(pltpu.make_async_copy(source, box, sems.at[2 * i]))
        if target is not None:
            stores.append(pltpu.make_async_copy(box, target, sems.at[2 * i + 1]))
        loads[-1].start()
    loads[0].wait()
    lines = norm_out.shape[0]
    norm_out[...] = gains_box[0:lines, :]
    query_out[...] = gains_box[lines : lines + 1, :]
    key_out[...] = gains_box[lines + 1 : lines + 2, :]
    for load, store in zip(loads[1:], stores):
        load.wait()
        store.start()
    for store in stores:
        store.wait()


def finish(context, token_grads, projection_grads, gains):
    width = HEAD_WIDTH
    vmem = pl.BlockSpec(memory_space=pltpu.VMEM)
    hbm = pl.BlockSpec(memory_space=pltpu.HBM)
    f32 = jnp.float32
    arrays = (context, token_grads, projection_grads)
    return pl.pallas_call(
        finish_kernel,
        out_shape=tuple(jax.ShapeDtypeStruct(array.shape, array.dtype) for array in arrays)
        + (
            jax.ShapeDtypeStruct((token_grads.shape[1] // width, width), f32),
            jax.ShapeDtypeStruct((1, width), f32),
            jax.ShapeDtypeStruct((1, width), f32),
        ),
        in_specs=[hbm] * 4,
        out_specs=(hbm,) * 3 + (vmem,) * 3,
        scratch_shapes=[pltpu.VMEM(array.shape, array.dtype) for array in arrays + (gains,)]
        + [pltpu.SemaphoreType.DMA((8,))],
        compiler_params=pltpu.CompilerParams(vmem_limit_bytes=60 * 1024 * 1024),
    )(*arrays, gains)


def rope_waves(local, blocks, width):
    half = width // 2
    frequency = THETA ** (-2.0 * np.arange(half) / width)
    frequency = np.concatenate([frequency, frequency])
    sign = np.concatenate([-np.ones(half), np.ones(half)])
    near = np.arange(local)[:, None] * frequency[None, :]
    far = np.arange(blocks)[:, None] * float(local) * frequency[None, :]
    waves = [np.cos(near), np.sin(near), np.cos(far), np.sin(far), sign * np.cos(far), sign * np.sin(far)]
    return np.concatenate(waves, axis=0).astype(np.float32)


def on_device(tokens, projection, norm_gain, query_gain, key_gain, segment_ids, context_cotangent):
    local = context_cotangent.shape[0]
    waves = jnp.asarray(rope_waves(local, SIDE * SIDE, HEAD_WIDTH))
    norm_gain = norm_gain.reshape(1, -1)
    query_gain = query_gain.reshape(1, -1)
    key_gain = key_gain.reshape(1, -1)
    segments = segment_ids.reshape(-1, 128)
    context, token_grads, projection_grads, gains = layer(
        tokens, projection, norm_gain, query_gain, key_gain, segments, waves, context_cotangent
    )
    context, token_grads, projection_grads, norm_gains, query_gains, key_gains = finish(
        context, token_grads, projection_grads, gains
    )
    return (
        context,
        token_grads,
        projection_grads,
        norm_gains.reshape(-1),
        query_gains.reshape(-1),
        key_gains.reshape(-1),
    )


def solution(mesh):
    placed = (
        P(("dp", "ctx", "tp"), None),
        P("ctx", "tp"),
        P(),
        P(),
        P(),
        P("dp"),
        P(("dp", "ctx"), "tp"),
    )
    return jax.shard_map(
        on_device,
        mesh=mesh,
        in_specs=placed,
        out_specs=(
            P(("dp", "ctx"), "tp"),
            P(("dp", "ctx", "tp"), None),
            P(("dp", "ctx"), "tp"),
            P("dp"),
            P("dp"),
            P("dp"),
        ),
        check_vma=False,
    )
```

```python
import jax
import jax.numpy as jnp
import numpy as np
from jax import lax
from jax.experimental import pallas as pl
from jax.experimental.pallas import tpu as pltpu
from jax.sharding import PartitionSpec as P

HEAD_WIDTH = 128
QUERY_PER_KEY = 4
SEGMENTS = 16
SIDE = 4
EPSILON = 1e-06
THETA = 1000000.0
LOG2E = 1.4426950408889634
MESH = pl.DeviceIdType.MESH
NT = (((1,), (1,)), ((), ()))
TN = (((0,), (0,)), ((), ()))


def wrap(value):
    return lax.rem(value + 2 * SIDE, SIDE)


def part_of(step):
    return 0 if step == 1 else 1


class Torus:
    def __init__(self, send_sems, recv_sems):
        ctx, tp = lax.axis_index("ctx"), lax.axis_index("tp")
        self.place = {
            "y": lax.div(ctx, SIDE),
            "x": lax.rem(ctx, SIDE),
            "z": lax.div(tp, 2),
            "core": lax.rem(tp, 2),
        }
        self.tp = tp
        self.sems = (send_sems, recv_sems)
        self.sent = []

    def along(self, axis, step):
        at = self.place
        if axis == "x":
            return {"ctx": at["y"] * SIDE + wrap(at["x"] + step)}
        if axis == "y":
            return {"ctx": wrap(at["y"] + step) * SIDE + at["x"]}
        if axis == "z":
            return {"tp": wrap(at["z"] + step) * 2 + at["core"]}
        return {"tp": at["z"] * 2 + 1 - at["core"]}

    def greet(self, steps):
        barrier = pltpu.get_barrier_semaphore()
        partners = [(axis, step) for axis in ("x", "y", "z") for step in steps] + [("core", 1)]
        for axis, step in partners:
            pl.semaphore_signal(
                barrier, inc=1, device_id=self.along(axis, step), device_id_type=MESH
            )
        pl.semaphore_wait(barrier, len(partners))

    def copy(self, index, source, target, axis, step):
        return pltpu.make_async_remote_copy(
            src_ref=source,
            dst_ref=target,
            send_sem=self.sems[0].at[index],
            recv_sem=self.sems[1].at[index],
            device_id=self.along(axis, step),
            device_id_type=MESH,
        )

    def send(self, source, target, axis, step):
        index = len(self.sent)
        copy = self.copy(index, source, target, axis, step)
        copy.start()
        self.sent.append(copy)
        return index

    def arrive(self, index, target):
        self.copy(index, target, target, "core", 1).wait_recv()

    def close(self):
        for copy in self.sent:
            copy.wait_send()


class Blocks:
    def __init__(self, torus, data, orders):
        self.torus, self.data, self.orders = torus, data, orders
        self.rows = data.shape[0] // (SIDE * SIDE)
        self.keys = {}

    def at(self, half, first, second, part=None):
        offset = dict(zip(self.orders[half], (first, second)))
        place = self.torus.place
        block = wrap(place["y"] + offset["y"]) * SIDE + wrap(place["x"] + offset["x"])
        rows = self.rows
        start = block * rows + half * (rows // 2)
        if part is not None:
            start = start + part * (rows // 4)
        size = rows // 2 if part is None else rows // 4
        return self.data.at[pl.ds(pl.multiple_of(start, rows // 4), size), :]

    def send(self, key, source, target, axis, step):
        self.keys[key] = self.torus.send(source, target, axis, step)

    def arrive(self, key, target):
        self.torus.arrive(self.keys[key], target)


class Gather(Blocks):
    def __init__(self, torus, data):
        super().__init__(torus, data, (("x", "y"), ("y", "x")))

    def pass_on(self, half, first):
        for step in (1, -1):
            block = self.at(half, first, 0)
            self.send(("q", half, first, step), block, block, self.orders[half][1], step)

    def start(self):
        for half in (0, 1):
            for step in (1, -1):
                block = self.at(half, 0, 0)
                self.send(("p", half, step), block, block, self.orders[half][0], step)
        for half in (0, 1):
            self.pass_on(half, 0)

    def near(self):
        for half in (0, 1):
            for step in (1, -1):
                self.arrive(("p", half, step), self.at(half, -step, 0))
                block = self.at(half, -step, 0, part_of(step))
                self.send(("f", half, step), block, block, self.orders[half][0], step)
        for half in (0, 1):
            for step in (1, -1):
                self.pass_on(half, -step)

    def far(self):
        for half in (0, 1):
            for step in (1, -1):
                self.arrive(("f", half, step), self.at(half, 2, 0, part_of(step)))
            self.pass_on(half, 2)

    def cross(self, firsts):
        for first in firsts:
            for half in (0, 1):
                for step in (1, -1):
                    self.arrive(("q", half, first, step), self.at(half, first, -step))
                    block = self.at(half, first, -step, part_of(step))
                    self.send(("g", half, first, step), block, block, self.orders[half][1], step)

    def finish(self):
        for first in (0, -1, 1, 2):
            for half in (0, 1):
                for step in (1, -1):
                    self.arrive(("g", half, first, step), self.at(half, first, 2, part_of(step)))


def add_to(target, *sources):
    total = target[...].astype(jnp.float32)
    for source in sources:
        total = total + source[...].astype(jnp.float32)
    target[...] = total.astype(target.dtype)


class Scatter(Blocks):
    def __init__(self, torus, data, far_one, near_one, far_two, near_two):
        super().__init__(torus, data, (("y", "x"), ("x", "y")))
        self.far_one, self.near_one = far_one, near_one
        self.far_two, self.near_two = far_two, near_two

    def start(self, halves=(0, 1)):
        for second in (2, 1, -1, 0):
            for half in halves:
                for step in (1, -1):
                    self.send(
                        ("f1", half, second, step),
                        self.at(half, 2, second, part_of(step)),
                        self.far_one.at[half, second % SIDE, part_of(step)],
                        self.orders[half][0],
                        step,
                    )

    def turn(self, seconds=(2, 1, -1, 0), steps=(1, -1)):
        for second in seconds:
            for half in (0, 1):
                for step in steps:
                    landed = self.far_one.at[half, second % SIDE, part_of(step)]
                    self.arrive(("f1", half, second, step), landed)
                    add_to(self.at(half, step, second, part_of(step)), landed)
                    self.send(
                        ("n1", half, second, step),
                        self.at(half, step, second),
                        self.near_one.at[half, second % SIDE, part_of(step)],
                        self.orders[half][0],
                        step,
                    )

    def land(self, seconds=(2, 1, -1, 0)):
        for second in seconds:
            for half in (0, 1):
                landed = [self.near_one.at[half, second % SIDE, part] for part in (0, 1)]
                for step in (1, -1):
                    self.arrive(("n1", half, second, step), landed[part_of(step)])
                add_to(self.at(half, 0, second), *landed)
                if second == 2:
                    for step in (1, -1):
                        self.send(
                            ("f2", half, step),
                            self.at(half, 0, 2, part_of(step)),
                            self.far_two.at[half, part_of(step)],
                            self.orders[half][1],
                            step,
                        )

    def turn_two(self):
        for half in (0, 1):
            for step in (1, -1):
                landed = self.far_two.at[half, part_of(step)]
                self.arrive(("f2", half, step), landed)
                add_to(self.at(half, 0, step, part_of(step)), landed)
                self.send(
                    ("n2", half, step),
                    self.at(half, 0, step),
                    self.near_two.at[half, part_of(step)],
                    self.orders[half][1],
                    step,
                )

    def finish(self, store):
        for half in (0, 1):
            landed = [self.near_two.at[half, part] for part in (0, 1)]
            for step in (1, -1):
                self.arrive(("n2", half, step), landed[part_of(step)])
            total = self.at(half, 0, 0)[...].astype(jnp.float32)
            for source in landed:
                total = total + source[...].astype(jnp.float32)
            store(slice(half * (self.rows // 2), (half + 1) * (self.rows // 2)), total)


def scatter_scratch(rows, columns):
    return [
        pltpu.VMEM((2, SIDE, 2, rows // 4, columns), jnp.bfloat16),
        pltpu.VMEM((2, SIDE, 2, rows // 2, columns), jnp.bfloat16),
        pltpu.VMEM((2, 2, rows // 4, columns), jnp.bfloat16),
        pltpu.VMEM((2, 2, rows // 2, columns), jnp.bfloat16),
    ]


def inverse_rms(values):
    return lax.rsqrt(jnp.mean(values * values, axis=-1, keepdims=True) + EPSILON)


def turn_halves(values):
    return pltpu.roll(values, HEAD_WIDTH // 2, 1)


def head_map(raw, gain, cosine, sine):
    scaled = raw * inverse_rms(raw) * gain
    return scaled * cosine + turn_halves(scaled) * sine


def head_map_back(raw, gain, cosine, sine, grads):
    inverse = inverse_rms(raw)
    unit = raw * inverse
    turned = grads * cosine + turn_halves(grads * sine)
    gain_grads = jnp.sum(turned * unit, axis=0, keepdims=True)
    scaled = turned * gain
    raw_grads = inverse * (scaled - unit * jnp.mean(scaled * unit, axis=-1, keepdims=True))
    return raw_grads, gain_grads


def layer_kernel(
    tokens_hbm, shard_hbm, norm_gain_hbm, query_gain_hbm, key_gain_hbm, segments_hbm, waves_hbm, up_hbm,
    context_ref, token_grads_ref, projection_grads_ref, gains_ref,
    send_sems, recv_sems, local_sems,
    tokens_ref, norm_gain_ref, query_gain_ref, key_gain_ref, segments_ref, waves_ref, up_ref,
    kv_ref, raw_ref, normed_ref, wkv_ref, wqa_ref, wqb_ref, rope_ref, bound_ref,
    exp_ref, q4_ref, q4t_ref, up4_ref, up4t_ref, num_ref, den_ref, corr_ref, dq_ref,
    dkv_ref, jq_ref, jkv_ref, gq_ref, gkv_ref, dkv_sum_ref,
    terms_ref, pair_ref, zfar_ref, znear_ref, gx_ref, gy_ref, gz_ref, gc_ref,
    *boxes,
):
    width = HEAD_WIDTH
    split = QUERY_PER_KEY * width
    pair_width = 2 * width
    torus = Torus(send_sems, recv_sems)
    rows = shard_hbm.shape[0]
    ctx = lax.axis_index("ctx")
    own = pl.ds(pl.multiple_of(ctx * rows, rows), rows)
    moves = (
        (shard_hbm.at[:, 0:pair_width], wqa_ref.at[own, :]),
        (tokens_hbm, tokens_ref),
        (norm_gain_hbm, norm_gain_ref),
        (shard_hbm.at[:, split:], wkv_ref.at[own, :]),
        (shard_hbm.at[:, pair_width:split], wqb_ref.at[own, :]),
        (waves_hbm, waves_ref),
        (segments_hbm, segments_ref),
        (query_gain_hbm, query_gain_ref),
        (key_gain_hbm, key_gain_ref),
        (up_hbm, up_ref),
    )
    loads = [
        pltpu.make_async_copy(source, target, local_sems.at[i])
        for i, (source, target) in enumerate(moves)
    ]
    for load in loads:
        load.start()
    torus.greet((1, 2, 3))
    loads[0].wait()
    weights_qa = Gather(torus, wqa_ref)
    weights_kv = Gather(torus, wkv_ref)
    weights_qb = Gather(torus, wqb_ref)
    keys_values = Gather(torus, kv_ref)
    weights_qa.start()

    count = tokens_ref.shape[0]

    def token_rows(step, part=None, flip=False):
        core = torus.place["core"]
        index = wrap(torus.place["z"] + step) * 2 + (1 - core if flip else core)
        size = count if part is None else count // 2
        start = index * count + (0 if part is None else part * (count // 2))
        return normed_ref.at[pl.ds(pl.multiple_of(start, count // 2), size), :]

    loads[1].wait()
    loads[2].wait()
    tokens = tokens_ref[...].astype(jnp.float32)
    token_rows(0)[...] = (tokens * inverse_rms(tokens) * norm_gain_ref[...]).astype(jnp.bfloat16)
    mine = token_rows(0)
    ring = {step: torus.send(mine, mine, "z", step) for step in (1, -1)}
    pair = {0: torus.send(mine, mine, "core", 1)}

    loads[3].wait()
    weights_kv.start()
    weights_qa.near()
    loads[4].wait()
    weights_qb.start()
    for load in loads[5:]:
        load.wait()
    local = rope_ref.shape[1]
    near_cosine, near_sine = waves_ref[0:local, :], waves_ref[local : 2 * local, :]

    def far_wave(i):
        return waves_ref[pl.ds(2 * local + i * SIDE * SIDE + ctx, 1), :]

    rope_ref[0] = far_wave(0) * near_cosine - far_wave(1) * near_sine
    rope_ref[1] = far_wave(3) * near_cosine + far_wave(2) * near_sine
    onward = {}
    for step in (1, -1):
        torus.arrive(ring[step], token_rows(-step))
        piece = token_rows(-step, part_of(step))
        onward[step] = torus.send(piece, piece, "z", step)
        block = token_rows(-step)
        pair[-step] = torus.send(block, block, "core", 1)
    weights_qa.far()
    for step in (1, -1):
        torus.arrive(onward[step], token_rows(2, part_of(step)))
    block = token_rows(2)
    pair[2] = torus.send(block, block, "core", 1)
    weights_qa.cross((0, -1, 1))
    weights_kv.near()
    weights_qa.cross((2,))

    segments = segments_ref[...]
    lines = local // segments.shape[1]
    for line in range(lines):
        asked = segments_ref[pl.ds(ctx * lines + line, 1), :]
        first = jnp.zeros(asked.shape, jnp.float32)
        last = jnp.zeros(asked.shape, jnp.float32)
        for number in range(SEGMENTS):
            size = jnp.where(segments == number, 1.0, 0.0)
            size = jnp.sum(jnp.sum(size, axis=0, keepdims=True), axis=1, keepdims=True)
            first = first + jnp.where(asked > number, size, 0.0)
            last = last + jnp.where(asked >= number, size, 0.0)
        columns = slice(line * segments.shape[1], (line + 1) * segments.shape[1])
        bound_ref[0:1, columns] = first
        bound_ref[1:2, columns] = last

    weights_kv.far()
    for step in (0, -1, 1, 2):
        torus.arrive(pair[step], token_rows(step, flip=True))
    weights_qa.finish()
    cosine, sine = rope_ref[0], rope_ref[1]

    def query_heads(weights_ref, heads):
        both = jnp.dot(normed_ref[...], weights_ref[...], preferred_element_type=jnp.float32)
        for i, g in enumerate(heads):
            raw = both[:, i * width : (i + 1) * width]
            raw_ref[:, g * width : (g + 1) * width] = raw
            query = head_map(raw, query_gain_ref[...], cosine, sine).astype(jnp.bfloat16)
            q4_ref[g] = query
            q4t_ref[g] = query.T

    weights_kv.cross((0, -1, 1))
    weights_qb.near()
    weights_kv.cross((2,))
    query_heads(wqa_ref, (0, 1))
    weights_qb.far()
    weights_kv.finish()
    raw = jnp.dot(normed_ref[...], wkv_ref[...], preferred_element_type=jnp.float32)
    raw_ref[:, split:] = raw[:, :width]
    kv_ref[own, 0:width] = head_map(raw[:, :width], key_gain_ref[...], cosine, sine).astype(
        jnp.bfloat16
    )
    kv_ref[own, width:] = raw[:, width:].astype(jnp.bfloat16)
    weights_qb.cross((0, -1, 1))
    keys_values.start()
    weights_qb.cross((2,))
    keys_values.near()
    weights_qb.finish()
    scale = width ** (-0.5)
    half_rows = local // 2
    start_row, end_row = bound_ref[0:1, :], bound_ref[1:2, :]
    num_ref[...] = jnp.zeros_like(num_ref)
    den_ref[...] = jnp.zeros_like(den_ref)
    dq_ref[...] = jnp.zeros_like(dq_ref)

    def pieces(half, offset):
        across = wrap(torus.place["y"] + offset) * SIDE * (1 - half)
        base = across + wrap(torus.place["x"] + offset) * half
        stride = 1 + (SIDE - 1) * half
        return [
            pl.multiple_of((base + i * stride) * local + half * half_rows, half_rows)
            for i in range(SIDE)
        ]

    def both_halves(step, offset):
        def body(half, carry):
            step(half, offset)
            return carry

        lax.fori_loop(0, 2, body, 0)

    def key_rows(starts):
        parts = [kv_ref[pl.ds(start, half_rows), :] for start in starts]
        both = jnp.concatenate(parts, axis=0)
        return both[:, 0:width], both[:, width:]

    def slot_of(half, offset):
        return half * SIDE + offset % SIDE

    def forward(half, offset):
        starts = pieces(half, offset)
        key, value = key_rows(starts)
        line = lax.broadcasted_iota(jnp.int32, (half_rows, local), 0)
        place = jnp.concatenate([line + start for start in starts], axis=0).astype(jnp.float32)
        mask = (place >= start_row) & (place < end_row)
        for g in range(QUERY_PER_KEY):
            scores = jnp.dot(key, q4t_ref[g], preferred_element_type=jnp.float32)
            exponent = jnp.where(mask, jnp.exp2(scores * (scale * LOG2E)), 0.0)
            den_ref[g] += jnp.sum(exponent.reshape(SIDE * half_rows // 8, 8, local), axis=0)
            rounded = exponent.astype(jnp.bfloat16)
            exp_ref[slot_of(half, offset), g] = rounded
            num_ref[g] += lax.dot_general(rounded, value, TN, preferred_element_type=jnp.float32)

    def backward(half, offset):
        starts = pieces(half, offset)
        key, value = key_rows(starts)
        dk = jnp.zeros((SIDE * half_rows, width), jnp.float32)
        dv = jnp.zeros((SIDE * half_rows, width), jnp.float32)
        for g in range(QUERY_PER_KEY):
            grads = jnp.dot(value, up4t_ref[g], preferred_element_type=jnp.float32)
            rounded = exp_ref[slot_of(half, offset), g]
            ds = (rounded.astype(jnp.float32) * (grads - corr_ref[g])).astype(jnp.bfloat16)
            dk += jnp.dot(ds, q4_ref[g], preferred_element_type=jnp.float32)
            dv += jnp.dot(rounded, up4_ref[g], preferred_element_type=jnp.float32)
            dq_ref[:, g * width : (g + 1) * width] += lax.dot_general(
                ds, key, TN, preferred_element_type=jnp.float32
            )
        for i, start in enumerate(starts):
            rows_here = slice(i * half_rows, (i + 1) * half_rows)
            at = pl.ds(start, half_rows)
            dkv_ref[at, 0:width] = (dk[rows_here] * scale).astype(jnp.bfloat16)
            dkv_ref[at, width:] = dv[rows_here].astype(jnp.bfloat16)

    keys_values.far()
    query_heads(wqb_ref, (2, 3))
    keys_values.cross((0, -1))
    both_halves(forward, 0)
    keys_values.cross((1, 2))
    both_halves(forward, -1)
    both_halves(forward, 1)
    keys_values.finish()
    both_halves(forward, 2)

    for g in range(QUERY_PER_KEY):
        columns = slice(g * width, (g + 1) * width)
        inverse = 1.0 / jnp.sum(den_ref[g].T, axis=1, keepdims=True)
        context = (num_ref[g] * inverse).astype(jnp.bfloat16)
        context_ref[:, columns] = context
        up = (up_ref[:, columns].astype(jnp.float32) * inverse).astype(jnp.bfloat16)
        up4_ref[g] = up
        up4t_ref[g] = up.T
        product = up.astype(jnp.float32) * context.astype(jnp.float32)
        corr_ref[g] = jnp.sum(product.T, axis=0, keepdims=True)

    dkv = Scatter(torus, dkv_ref, *boxes[0:4])
    dwq = Scatter(torus, gq_ref, *boxes[4:8])
    dwkv = Scatter(torus, gkv_ref, *boxes[8:12])
    both_halves(backward, 2)
    dkv.start()
    for offset in (1, -1):
        both_halves(backward, offset)
        dkv.turn(steps=(offset,))
    both_halves(backward, 0)
    dkv.land()

    query_gain_grads = jnp.zeros((1, width), jnp.float32)
    for g in range(QUERY_PER_KEY):
        columns = slice(g * width, (g + 1) * width)
        raw_grads, gain_grads = head_map_back(
            raw_ref[:, columns], query_gain_ref[...], cosine, sine, dq_ref[:, columns] * scale
        )
        jq_ref[:, columns] = raw_grads.astype(jnp.bfloat16)
        query_gain_grads = query_gain_grads + gain_grads

    def weight_grads(j_ref, g_ref):
        def piece(half, offset):
            starts = pieces(half, offset)
            rows = jnp.concatenate(
                [normed_ref[:, pl.ds(start, half_rows)] for start in starts], axis=1
            )
            grads = lax.dot_general(rows, j_ref[...], TN, preferred_element_type=jnp.float32)
            for i, start in enumerate(starts):
                g_ref[pl.ds(start, half_rows), :] = grads[
                    i * half_rows : (i + 1) * half_rows
                ].astype(jnp.bfloat16)

        return piece

    query_weights = weight_grads(jq_ref, gq_ref)
    both_halves(query_weights, 2)
    dwq.start()
    dkv.turn_two()
    for offset in (1, -1, 0):
        both_halves(query_weights, offset)

    def query_terms(i, carry):
        at = pl.ds(pl.multiple_of(i * 256, 256), 256)
        terms_ref[:, at] = (
            lax.dot_general(
                jq_ref[:, 0:pair_width], wqa_ref[at, :], NT, preferred_element_type=jnp.float32
            )
            + lax.dot_general(
                jq_ref[:, pair_width:], wqb_ref[at, :], NT, preferred_element_type=jnp.float32
            )
        ).astype(jnp.bfloat16)
        return carry

    lax.fori_loop(0, terms_ref.shape[1] // 256, query_terms, 0)

    def keep_dkv(at, total):
        dkv_sum_ref[at, :] = total

    dkv.finish(keep_dkv)
    raw_grads, key_gain_grads = head_map_back(
        raw_ref[:, split:], key_gain_ref[...], cosine, sine, dkv_sum_ref[:, :width]
    )
    jkv_ref[:, :width] = raw_grads.astype(jnp.bfloat16)
    jkv_ref[:, width:] = dkv_sum_ref[:, width:].astype(jnp.bfloat16)
    pair_weights = weight_grads(jkv_ref, gkv_ref)
    both_halves(pair_weights, 2)
    dwkv.start()

    def value_terms(i, carry):
        at = pl.ds(pl.multiple_of(i * 256, 256), 256)
        terms_ref[:, at] = (
            terms_ref[:, at].astype(jnp.float32)
            + lax.dot_general(jkv_ref[...], wkv_ref[at, :], NT, preferred_element_type=jnp.float32)
        ).astype(jnp.bfloat16)
        return carry

    def term_rows(step, part=None, flip=False):
        core = torus.place["core"]
        index = wrap(torus.place["z"] + step) * 2 + (1 - core if flip else core)
        size = count if part is None else count // 2
        start = index * count + (0 if part is None else part * (count // 2))
        return terms_ref.at[pl.ds(pl.multiple_of(start, count // 2), size), :]

    dwq.turn((2, 1))
    lax.fori_loop(0, terms_ref.shape[1] // 256, value_terms, 0)
    pair = {
        step: torus.send(term_rows(step, flip=True), pair_ref.at[step % SIDE], "core", 1)
        for step in (2, 1, -1, 0)
    }
    dwq.turn((-1, 0))
    for offset in (1, -1, 0):
        both_halves(pair_weights, offset)
    torus.arrive(pair[2], pair_ref.at[2])
    add_to(term_rows(2), pair_ref.at[2])
    far = {}
    for step in (1, -1):
        far[step] = torus.send(
            term_rows(2, part_of(step)), zfar_ref.at[part_of(step)], "z", step
        )
    dwkv.turn()
    for step in (1, -1):
        torus.arrive(pair[step], pair_ref.at[step % SIDE])
        add_to(term_rows(step), pair_ref.at[step % SIDE])
    dwq.land((2,))
    near = {}
    for step in (1, -1):
        torus.arrive(far[step], zfar_ref.at[part_of(step)])
        add_to(term_rows(step, part_of(step)), zfar_ref.at[part_of(step)])
        near[step] = torus.send(term_rows(step), znear_ref.at[part_of(step)], "z", step)
    dwq.land((1, -1))
    dwq.turn_two()
    torus.arrive(pair[0], pair_ref.at[0])
    for step in (1, -1):
        torus.arrive(near[step], znear_ref.at[part_of(step)])
    normed_grads = term_rows(0)[...].astype(jnp.float32) + pair_ref[0].astype(jnp.float32)
    normed_grads = normed_grads + (
        znear_ref[0].astype(jnp.float32) + znear_ref[1].astype(jnp.float32)
    )
    tokens = tokens_ref[...].astype(jnp.float32)
    inverse = inverse_rms(tokens)
    unit = tokens * inverse
    norm_gain_grads = jnp.sum(normed_grads * unit, axis=0, keepdims=True)
    scaled = normed_grads * norm_gain_ref[...]
    token_grads_ref[...] = inverse * (
        scaled - unit * jnp.mean(scaled * unit, axis=-1, keepdims=True)
    )
    lines = tokens.shape[1] // width
    gains_ref[...] = jnp.zeros_like(gains_ref)
    for i in range(lines):
        gains_ref[i : i + 1, :] = norm_gain_grads[:, i * width : (i + 1) * width]
    gains_ref[lines : lines + 1, :] = query_gain_grads
    gains_ref[lines + 1 : lines + 2, :] = key_gain_grads

    def share(axis, box):
        place, size = torus.place[axis], box.shape[0]
        box[place] = gains_ref[...]
        return [
            torus.send(box.at[place], box.at[place], axis, step) for step in range(1, size)
        ]

    def collect(axis, box, sent):
        place, size = torus.place[axis], box.shape[0]
        for step in range(1, size):
            torus.arrive(sent[step - 1], box.at[lax.rem(place + size - step, size)])
        total = box[0]
        for i in range(1, size):
            total = total + box[i]
        gains_ref[...] = total

    def keep_q(at, total):
        projection_grads_ref[at, :split] = total

    def keep_kv(at, total):
        projection_grads_ref[at, split:] = total

    sent = share("z", gz_ref)
    dwq.land((0,))
    dwkv.land((2,))
    collect("z", gz_ref, sent)
    sent = share("core", gc_ref)
    dwkv.land((1, -1))
    collect("core", gc_ref, sent)
    sent = share("x", gx_ref)
    dwkv.turn_two()
    collect("x", gx_ref, sent)
    sent = share("y", gy_ref)
    dwq.finish(keep_q)
    dwkv.land((0,))
    dwkv.finish(keep_kv)
    collect("y", gy_ref, sent)
    torus.close()


def layer(tokens, shard, norm_gain, query_gain, key_gain, segments, waves, upstream):
    rows, columns = shard.shape
    count, depth = tokens.shape
    local = upstream.shape[0]
    total = local * SIDE * SIDE
    group, width = QUERY_PER_KEY, HEAD_WIDTH
    split = group * width
    gains = (depth // width + 8, width)
    copies = 7 * 40 + 8 + 8 + 10
    bf16, f32 = jnp.bfloat16, jnp.float32
    vmem = pl.BlockSpec(memory_space=pltpu.VMEM)
    hbm = pl.BlockSpec(memory_space=pltpu.HBM)
    return pl.pallas_call(
        layer_kernel,
        out_shape=(
            jax.ShapeDtypeStruct((local, split), bf16),
            jax.ShapeDtypeStruct((count, depth), f32),
            jax.ShapeDtypeStruct((rows, columns), f32),
            jax.ShapeDtypeStruct(gains, f32),
        ),
        in_specs=[hbm] * 8,
        out_specs=(vmem,) * 4,
        scratch_shapes=[
            pltpu.SemaphoreType.DMA((copies,)),
            pltpu.SemaphoreType.DMA((copies,)),
            pltpu.SemaphoreType.DMA((10,)),
            pltpu.VMEM(tokens.shape, bf16),
            pltpu.VMEM(norm_gain.shape, f32),
            pltpu.VMEM(query_gain.shape, f32),
            pltpu.VMEM(key_gain.shape, f32),
            pltpu.VMEM(segments.shape, jnp.int32),
            pltpu.VMEM(waves.shape, f32),
            pltpu.VMEM(upstream.shape, bf16),
            pltpu.VMEM((total, 2 * width), bf16),
            pltpu.VMEM((local, split + width), f32),
            pltpu.VMEM((local, depth), bf16),
            pltpu.VMEM((depth, 2 * width), bf16),
            pltpu.VMEM((depth, split // 2), bf16),
            pltpu.VMEM((depth, split // 2), bf16),
            pltpu.VMEM((2, local, width), f32),
            pltpu.VMEM((2, local), f32),
            pltpu.VMEM((2 * SIDE, group, total // (2 * SIDE), local), bf16),
            pltpu.VMEM((group, local, width), bf16),
            pltpu.VMEM((group, width, local), bf16),
            pltpu.VMEM((group, local, width), bf16),
            pltpu.VMEM((group, width, local), bf16),
            pltpu.VMEM((group, local, width), f32),
            pltpu.VMEM((group, 8, local), f32),
            pltpu.VMEM((group, 1, local), f32),
            pltpu.VMEM((local, split), f32),
            pltpu.VMEM((total, 2 * width), bf16),
            pltpu.VMEM((local, split), bf16),
            pltpu.VMEM((local, 2 * width), bf16),
            pltpu.VMEM((depth, split), bf16),
            pltpu.VMEM((depth, 2 * width), bf16),
            pltpu.VMEM((local, 2 * width), f32),
            pltpu.VMEM((local, depth), bf16),
            pltpu.VMEM((SIDE, count, depth), bf16),
            pltpu.VMEM((2, count // 2, depth), bf16),
            pltpu.VMEM((2, count, depth), bf16),
            pltpu.VMEM((SIDE,) + gains, f32),
            pltpu.VMEM((SIDE,) + gains, f32),
            pltpu.VMEM((SIDE,) + gains, f32),
            pltpu.VMEM((2,) + gains, f32),
        ]
        + scatter_scratch(local, 2 * width)
        + scatter_scratch(rows, split)
        + scatter_scratch(rows, 2 * width),
        compiler_params=pltpu.CompilerParams(
            collective_id=0, has_side_effects=True, vmem_limit_bytes=60 * 1024 * 1024
        ),
        cost_estimate=pl.CostEstimate(
            flops=6 * local * depth * columns + 14 * group * local * total * width,
            bytes_accessed=8 * depth * columns,
            transcendentals=group * local * total,
        ),
    )(tokens, shard, norm_gain, query_gain, key_gain, segments, waves, upstream)


def finish_kernel(
    context_ref, token_ref, projection_ref, gains_ref,
    context_out, token_out, projection_out, norm_out, query_out, key_out,
    context_box, token_box, projection_box, gains_box, sems,
):
    loads, stores = [], []
    for i, (source, box, target) in enumerate(
        (
            (gains_ref, gains_box, None),
            (projection_ref, projection_box, projection_out),
            (token_ref, token_box, token_out),
            (context_ref, context_box, context_out),
        )
    ):
        loads.append(pltpu.make_async_copy(source, box, sems.at[2 * i]))
        if target is not None:
            stores.append(pltpu.make_async_copy(box, target, sems.at[2 * i + 1]))
        loads[-1].start()
    loads[0].wait()
    lines = norm_out.shape[0]
    norm_out[...] = gains_box[0:lines, :]
    query_out[...] = gains_box[lines : lines + 1, :]
    key_out[...] = gains_box[lines + 1 : lines + 2, :]
    for load, store in zip(loads[1:], stores):
        load.wait()
        store.start()
    for store in stores:
        store.wait()


def finish(context, token_grads, projection_grads, gains):
    width = HEAD_WIDTH
    vmem = pl.BlockSpec(memory_space=pltpu.VMEM)
    hbm = pl.BlockSpec(memory_space=pltpu.HBM)
    f32 = jnp.float32
    arrays = (context, token_grads, projection_grads)
    return pl.pallas_call(
        finish_kernel,
        out_shape=tuple(jax.ShapeDtypeStruct(array.shape, array.dtype) for array in arrays)
        + (
            jax.ShapeDtypeStruct((token_grads.shape[1] // width, width), f32),
            jax.ShapeDtypeStruct((1, width), f32),
            jax.ShapeDtypeStruct((1, width), f32),
        ),
        in_specs=[hbm] * 4,
        out_specs=(hbm,) * 3 + (vmem,) * 3,
        scratch_shapes=[pltpu.VMEM(array.shape, array.dtype) for array in arrays + (gains,)]
        + [pltpu.SemaphoreType.DMA((8,))],
        compiler_params=pltpu.CompilerParams(vmem_limit_bytes=60 * 1024 * 1024),
    )(*arrays, gains)


def rope_waves(local, blocks, width):
    half = width // 2
    frequency = THETA ** (-2.0 * np.arange(half) / width)
    frequency = np.concatenate([frequency, frequency])
    sign = np.concatenate([-np.ones(half), np.ones(half)])
    near = np.arange(local)[:, None] * frequency[None, :]
    far = np.arange(blocks)[:, None] * float(local) * frequency[None, :]
    waves = [np.cos(near), np.sin(near), np.cos(far), np.sin(far), sign * np.cos(far), sign * np.sin(far)]
    return np.concatenate(waves, axis=0).astype(np.float32)


def on_device(tokens, projection, norm_gain, query_gain, key_gain, segment_ids, context_cotangent):
    local = context_cotangent.shape[0]
    waves = jnp.asarray(rope_waves(local, SIDE * SIDE, HEAD_WIDTH))
    norm_gain = norm_gain.reshape(1, -1)
    query_gain = query_gain.reshape(1, -1)
    key_gain = key_gain.reshape(1, -1)
    segments = segment_ids.reshape(-1, 128)
    context, token_grads, projection_grads, gains = layer(
        tokens, projection, norm_gain, query_gain, key_gain, segments, waves, context_cotangent
    )
    context, token_grads, projection_grads, norm_gains, query_gains, key_gains = finish(
        context, token_grads, projection_grads, gains
    )
    return (
        context,
        token_grads,
        projection_grads,
        norm_gains.reshape(-1),
        query_gains.reshape(-1),
        key_gains.reshape(-1),
    )


def solution(mesh):
    placed = (
        P(("dp", "ctx", "tp"), None),
        P("ctx", "tp"),
        P(),
        P(),
        P(),
        P("dp"),
        P(("dp", "ctx"), "tp"),
    )
    return jax.shard_map(
        on_device,
        mesh=mesh,
        in_specs=placed,
        out_specs=(
            P(("dp", "ctx"), "tp"),
            P(("dp", "ctx", "tp"), None),
            P(("dp", "ctx"), "tp"),
            P("dp"),
            P("dp"),
            P("dp"),
        ),
        check_vma=False,
    )
```

```python
import jax
import jax.numpy as jnp
import numpy as np
from jax import lax
from jax.experimental import pallas as pl
from jax.experimental.pallas import tpu as pltpu
from jax.sharding import PartitionSpec as P

HEAD_WIDTH = 128
QUERY_PER_KEY = 4
SEGMENTS = 16
SIDE = 4
EPSILON = 1e-06
THETA = 1000000.0
LOG2E = 1.4426950408889634
MESH = pl.DeviceIdType.MESH
NT = (((1,), (1,)), ((), ()))
TN = (((0,), (0,)), ((), ()))


def wrap(value):
    return lax.rem(value + 2 * SIDE, SIDE)


def part_of(step):
    return 0 if step == 1 else 1


class Torus:
    def __init__(self, send_sems, recv_sems):
        ctx, tp = lax.axis_index("ctx"), lax.axis_index("tp")
        self.place = {
            "y": lax.div(ctx, SIDE),
            "x": lax.rem(ctx, SIDE),
            "z": lax.div(tp, 2),
            "core": lax.rem(tp, 2),
        }
        self.tp = tp
        self.sems = (send_sems, recv_sems)
        self.sent = []

    def along(self, axis, step):
        at = self.place
        if axis == "x":
            return {"ctx": at["y"] * SIDE + wrap(at["x"] + step)}
        if axis == "y":
            return {"ctx": wrap(at["y"] + step) * SIDE + at["x"]}
        if axis == "z":
            return {"tp": wrap(at["z"] + step) * 2 + at["core"]}
        return {"tp": at["z"] * 2 + 1 - at["core"]}

    def greet(self, steps):
        barrier = pltpu.get_barrier_semaphore()
        partners = [(axis, step) for axis in ("x", "y", "z") for step in steps] + [("core", 1)]
        for axis, step in partners:
            pl.semaphore_signal(
                barrier, inc=1, device_id=self.along(axis, step), device_id_type=MESH
            )
        pl.semaphore_wait(barrier, len(partners))

    def copy(self, index, source, target, axis, step):
        return pltpu.make_async_remote_copy(
            src_ref=source,
            dst_ref=target,
            send_sem=self.sems[0].at[index],
            recv_sem=self.sems[1].at[index],
            device_id=self.along(axis, step),
            device_id_type=MESH,
        )

    def send(self, source, target, axis, step):
        index = len(self.sent)
        copy = self.copy(index, source, target, axis, step)
        copy.start()
        self.sent.append(copy)
        return index

    def arrive(self, index, target):
        self.copy(index, target, target, "core", 1).wait_recv()

    def close(self):
        for copy in self.sent:
            copy.wait_send()


class Blocks:
    def __init__(self, torus, data, orders):
        self.torus, self.data, self.orders = torus, data, orders
        self.rows = data.shape[0] // (SIDE * SIDE)
        self.keys = {}

    def at(self, half, first, second, part=None):
        offset = dict(zip(self.orders[half], (first, second)))
        place = self.torus.place
        block = wrap(place["y"] + offset["y"]) * SIDE + wrap(place["x"] + offset["x"])
        rows = self.rows
        start = block * rows + half * (rows // 2)
        if part is not None:
            start = start + part * (rows // 4)
        size = rows // 2 if part is None else rows // 4
        return self.data.at[pl.ds(pl.multiple_of(start, rows // 4), size), :]

    def send(self, key, source, target, axis, step):
        self.keys[key] = self.torus.send(source, target, axis, step)

    def arrive(self, key, target):
        self.torus.arrive(self.keys[key], target)


class Gather(Blocks):
    def __init__(self, torus, data):
        super().__init__(torus, data, (("x", "y"), ("y", "x")))

    def pass_on(self, half, first):
        for step in (1, -1):
            block = self.at(half, first, 0)
            self.send(("q", half, first, step), block, block, self.orders[half][1], step)

    def start(self):
        for half in (0, 1):
            for step in (1, -1):
                block = self.at(half, 0, 0)
                self.send(("p", half, step), block, block, self.orders[half][0], step)
        for half in (0, 1):
            self.pass_on(half, 0)

    def near(self):
        for half in (0, 1):
            for step in (1, -1):
                self.arrive(("p", half, step), self.at(half, -step, 0))
                block = self.at(half, -step, 0, part_of(step))
                self.send(("f", half, step), block, block, self.orders[half][0], step)
        for half in (0, 1):
            for step in (1, -1):
                self.pass_on(half, -step)

    def far(self):
        for half in (0, 1):
            for step in (1, -1):
                self.arrive(("f", half, step), self.at(half, 2, 0, part_of(step)))
            self.pass_on(half, 2)

    def cross(self, firsts):
        for first in firsts:
            for half in (0, 1):
                for step in (1, -1):
                    self.arrive(("q", half, first, step), self.at(half, first, -step))
                    block = self.at(half, first, -step, part_of(step))
                    self.send(("g", half, first, step), block, block, self.orders[half][1], step)

    def finish(self):
        for first in (0, -1, 1, 2):
            for half in (0, 1):
                for step in (1, -1):
                    self.arrive(("g", half, first, step), self.at(half, first, 2, part_of(step)))


def add_to(target, *sources):
    total = target[...].astype(jnp.float32)
    for source in sources:
        total = total + source[...].astype(jnp.float32)
    target[...] = total.astype(target.dtype)


class Scatter(Blocks):
    def __init__(self, torus, data, far_one, near_one, far_two, near_two):
        super().__init__(torus, data, (("y", "x"), ("x", "y")))
        self.far_one, self.near_one = far_one, near_one
        self.far_two, self.near_two = far_two, near_two

    def start(self, halves=(0, 1)):
        for second in (2, 1, -1, 0):
            for half in halves:
                for step in (1, -1):
                    self.send(
                        ("f1", half, second, step),
                        self.at(half, 2, second, part_of(step)),
                        self.far_one.at[half, second % SIDE, part_of(step)],
                        self.orders[half][0],
                        step,
                    )

    def turn(self, seconds=(2, 1, -1, 0), steps=(1, -1)):
        for second in seconds:
            for half in (0, 1):
                for step in steps:
                    landed = self.far_one.at[half, second % SIDE, part_of(step)]
                    self.arrive(("f1", half, second, step), landed)
                    add_to(self.at(half, step, second, part_of(step)), landed)
                    self.send(
                        ("n1", half, second, step),
                        self.at(half, step, second),
                        self.near_one.at[half, second % SIDE, part_of(step)],
                        self.orders[half][0],
                        step,
                    )

    def land(self, seconds=(2, 1, -1, 0)):
        for second in seconds:
            for half in (0, 1):
                landed = [self.near_one.at[half, second % SIDE, part] for part in (0, 1)]
                for step in (1, -1):
                    self.arrive(("n1", half, second, step), landed[part_of(step)])
                add_to(self.at(half, 0, second), *landed)
                if second == 2:
                    for step in (1, -1):
                        self.send(
                            ("f2", half, step),
                            self.at(half, 0, 2, part_of(step)),
                            self.far_two.at[half, part_of(step)],
                            self.orders[half][1],
                            step,
                        )

    def turn_two(self):
        for half in (0, 1):
            for step in (1, -1):
                landed = self.far_two.at[half, part_of(step)]
                self.arrive(("f2", half, step), landed)
                add_to(self.at(half, 0, step, part_of(step)), landed)
                self.send(
                    ("n2", half, step),
                    self.at(half, 0, step),
                    self.near_two.at[half, part_of(step)],
                    self.orders[half][1],
                    step,
                )

    def finish(self, store):
        for half in (0, 1):
            landed = [self.near_two.at[half, part] for part in (0, 1)]
            for step in (1, -1):
                self.arrive(("n2", half, step), landed[part_of(step)])
            total = self.at(half, 0, 0)[...].astype(jnp.float32)
            for source in landed:
                total = total + source[...].astype(jnp.float32)
            store(slice(half * (self.rows // 2), (half + 1) * (self.rows // 2)), total)


def scatter_scratch(rows, columns):
    return [
        pltpu.VMEM((2, SIDE, 2, rows // 4, columns), jnp.bfloat16),
        pltpu.VMEM((2, SIDE, 2, rows // 2, columns), jnp.bfloat16),
        pltpu.VMEM((2, 2, rows // 4, columns), jnp.bfloat16),
        pltpu.VMEM((2, 2, rows // 2, columns), jnp.bfloat16),
    ]


def inverse_rms(values):
    return lax.rsqrt(jnp.mean(values * values, axis=-1, keepdims=True) + EPSILON)


def turn_halves(values):
    return pltpu.roll(values, HEAD_WIDTH // 2, 1)


def head_map(raw, gain, cosine, sine):
    scaled = raw * inverse_rms(raw) * gain
    return scaled * cosine + turn_halves(scaled) * sine


def head_map_back(raw, gain, cosine, sine, grads):
    inverse = inverse_rms(raw)
    unit = raw * inverse
    turned = grads * cosine + turn_halves(grads * sine)
    gain_grads = jnp.sum(turned * unit, axis=0, keepdims=True)
    scaled = turned * gain
    raw_grads = inverse * (scaled - unit * jnp.mean(scaled * unit, axis=-1, keepdims=True))
    return raw_grads, gain_grads


def layer_kernel(
    tokens_hbm, shard_hbm, norm_gain_hbm, query_gain_hbm, key_gain_hbm, segments_hbm, waves_hbm, up_hbm,
    context_ref, token_grads_ref, projection_grads_ref, gains_ref,
    send_sems, recv_sems, local_sems,
    tokens_ref, norm_gain_ref, query_gain_ref, key_gain_ref, segments_ref, waves_ref, up_ref,
    kv_ref, raw_ref, normed_ref, wkv_ref, wqa_ref, wqb_ref, rope_ref, bound_ref,
    exp_ref, q4_ref, q4t_ref, up4_ref, up4t_ref, num_ref, den_ref, corr_ref, dq_ref,
    dkv_ref, jq_ref, jkv_ref, gq_ref, gkv_ref, dkv_sum_ref,
    terms_ref, pair_ref, zfar_ref, znear_ref, gx_ref, gy_ref, gz_ref, gc_ref,
    *boxes,
):
    width = HEAD_WIDTH
    split = QUERY_PER_KEY * width
    pair_width = 2 * width
    torus = Torus(send_sems, recv_sems)
    rows = shard_hbm.shape[0]
    ctx = lax.axis_index("ctx")
    own = pl.ds(pl.multiple_of(ctx * rows, rows), rows)
    moves = (
        (shard_hbm.at[:, 0:pair_width], wqa_ref.at[own, :]),
        (tokens_hbm, tokens_ref),
        (norm_gain_hbm, norm_gain_ref),
        (shard_hbm.at[:, split:], wkv_ref.at[own, :]),
        (shard_hbm.at[:, pair_width:split], wqb_ref.at[own, :]),
        (waves_hbm, waves_ref),
        (segments_hbm, segments_ref),
        (query_gain_hbm, query_gain_ref),
        (key_gain_hbm, key_gain_ref),
        (up_hbm, up_ref),
    )
    loads = [
        pltpu.make_async_copy(source, target, local_sems.at[i])
        for i, (source, target) in enumerate(moves)
    ]
    for load in loads:
        load.start()
    torus.greet((1, 2, 3))
    loads[0].wait()
    weights_qa = Gather(torus, wqa_ref)
    weights_kv = Gather(torus, wkv_ref)
    weights_qb = Gather(torus, wqb_ref)
    keys_values = Gather(torus, kv_ref)
    weights_qa.start()

    count = tokens_ref.shape[0]

    def token_rows(step, part=None, flip=False):
        core = torus.place["core"]
        index = wrap(torus.place["z"] + step) * 2 + (1 - core if flip else core)
        size = count if part is None else count // 2
        start = index * count + (0 if part is None else part * (count // 2))
        return normed_ref.at[pl.ds(pl.multiple_of(start, count // 2), size), :]

    loads[1].wait()
    loads[2].wait()
    tokens = tokens_ref[...].astype(jnp.float32)
    token_rows(0)[...] = (tokens * inverse_rms(tokens) * norm_gain_ref[...]).astype(jnp.bfloat16)
    mine = token_rows(0)
    ring = {step: torus.send(mine, mine, "z", step) for step in (1, -1)}
    pair = {0: torus.send(mine, mine, "core", 1)}

    loads[3].wait()
    weights_kv.start()
    weights_qa.near()
    loads[4].wait()
    weights_qb.start()
    for load in loads[5:]:
        load.wait()
    local = rope_ref.shape[1]
    near_cosine, near_sine = waves_ref[0:local, :], waves_ref[local : 2 * local, :]

    def far_wave(i):
        return waves_ref[pl.ds(2 * local + i * SIDE * SIDE + ctx, 1), :]

    rope_ref[0] = far_wave(0) * near_cosine - far_wave(1) * near_sine
    rope_ref[1] = far_wave(3) * near_cosine + far_wave(2) * near_sine
    onward = {}
    for step in (1, -1):
        torus.arrive(ring[step], token_rows(-step))
        piece = token_rows(-step, part_of(step))
        onward[step] = torus.send(piece, piece, "z", step)
        block = token_rows(-step)
        pair[-step] = torus.send(block, block, "core", 1)
    weights_qa.far()
    for step in (1, -1):
        torus.arrive(onward[step], token_rows(2, part_of(step)))
    block = token_rows(2)
    pair[2] = torus.send(block, block, "core", 1)
    weights_qa.cross((0, -1, 1))
    weights_kv.near()
    weights_qa.cross((2,))

    segments = segments_ref[...]
    lines = local // segments.shape[1]
    for line in range(lines):
        asked = segments_ref[pl.ds(ctx * lines + line, 1), :]
        first = jnp.zeros(asked.shape, jnp.float32)
        last = jnp.zeros(asked.shape, jnp.float32)
        for number in range(SEGMENTS):
            size = jnp.where(segments == number, 1.0, 0.0)
            size = jnp.sum(jnp.sum(size, axis=0, keepdims=True), axis=1, keepdims=True)
            first = first + jnp.where(asked > number, size, 0.0)
            last = last + jnp.where(asked >= number, size, 0.0)
        columns = slice(line * segments.shape[1], (line + 1) * segments.shape[1])
        bound_ref[0:1, columns] = first
        bound_ref[1:2, columns] = last

    weights_kv.far()
    for step in (0, -1, 1, 2):
        torus.arrive(pair[step], token_rows(step, flip=True))
    weights_qa.finish()
    cosine, sine = rope_ref[0], rope_ref[1]

    def query_heads(weights_ref, heads):
        both = jnp.dot(normed_ref[...], weights_ref[...], preferred_element_type=jnp.float32)
        for i, g in enumerate(heads):
            raw = both[:, i * width : (i + 1) * width]
            raw_ref[:, g * width : (g + 1) * width] = raw
            query = head_map(raw, query_gain_ref[...], cosine, sine).astype(jnp.bfloat16)
            q4_ref[g] = query
            q4t_ref[g] = query.T

    weights_kv.cross((0, -1, 1))
    weights_qb.near()
    weights_kv.cross((2,))
    query_heads(wqa_ref, (0, 1))
    weights_qb.far()
    weights_kv.finish()
    raw = jnp.dot(normed_ref[...], wkv_ref[...], preferred_element_type=jnp.float32)
    raw_ref[:, split:] = raw[:, :width]
    kv_ref[own, 0:width] = head_map(raw[:, :width], key_gain_ref[...], cosine, sine).astype(
        jnp.bfloat16
    )
    kv_ref[own, width:] = raw[:, width:].astype(jnp.bfloat16)
    weights_qb.cross((0, -1, 1))
    keys_values.start()
    weights_qb.cross((2,))
    keys_values.near()
    weights_qb.finish()
    scale = width ** (-0.5)
    half_rows = local // 2
    start_row, end_row = bound_ref[0:1, :], bound_ref[1:2, :]
    num_ref[...] = jnp.zeros_like(num_ref)
    den_ref[...] = jnp.zeros_like(den_ref)
    dq_ref[...] = jnp.zeros_like(dq_ref)

    def pieces(half, offset):
        if half is None:
            return pieces(0, offset) + pieces(1, offset)
        across = wrap(torus.place["y"] + offset) * SIDE * (1 - half)
        base = across + wrap(torus.place["x"] + offset) * half
        stride = 1 + (SIDE - 1) * half
        return [
            pl.multiple_of((base + i * stride) * local + half * half_rows, half_rows)
            for i in range(SIDE)
        ]

    def both_halves(step, offset):
        def body(half, carry):
            step(half, offset)
            return carry

        lax.fori_loop(0, 2, body, 0)

    def two_offsets(step, first):
        def body(i, carry):
            step(None, first - 2 * first * i)
            return carry

        lax.fori_loop(0, 2, body, 0)

    def key_rows(starts):
        parts = [kv_ref[pl.ds(start, half_rows), :] for start in starts]
        both = jnp.concatenate(parts, axis=0)
        return both[:, 0:width], both[:, width:]

    def slots_of(half, offset):
        return [side * SIDE + wrap(offset) for side in ((0, 1) if half is None else (half,))]

    def forward(half, offset):
        starts = pieces(half, offset)
        key, value = key_rows(starts)
        line = lax.broadcasted_iota(jnp.int32, (half_rows, local), 0)
        place = jnp.concatenate([line + start for start in starts], axis=0).astype(jnp.float32)
        mask = (place >= start_row) & (place < end_row)
        for g in range(QUERY_PER_KEY):
            scores = jnp.dot(key, q4t_ref[g], preferred_element_type=jnp.float32)
            exponent = jnp.where(mask, jnp.exp2(scores * (scale * LOG2E)), 0.0)
            den_ref[g] += jnp.sum(exponent.reshape(-1, 8, local), axis=0)
            rounded = exponent.astype(jnp.bfloat16)
            for i, slot in enumerate(slots_of(half, offset)):
                exp_ref[slot, g] = rounded[i * SIDE * half_rows : (i + 1) * SIDE * half_rows]
            num_ref[g] += lax.dot_general(rounded, value, TN, preferred_element_type=jnp.float32)

    def backward(half, offset):
        starts = pieces(half, offset)
        key, value = key_rows(starts)
        dk = jnp.zeros((len(starts) * half_rows, width), jnp.float32)
        dv = jnp.zeros((len(starts) * half_rows, width), jnp.float32)
        for g in range(QUERY_PER_KEY):
            grads = jnp.dot(value, up4t_ref[g], preferred_element_type=jnp.float32)
            rounded = jnp.concatenate(
                [exp_ref[slot, g] for slot in slots_of(half, offset)], axis=0
            )
            ds = (rounded.astype(jnp.float32) * (grads - corr_ref[g])).astype(jnp.bfloat16)
            dk += jnp.dot(ds, q4_ref[g], preferred_element_type=jnp.float32)
            dv += jnp.dot(rounded, up4_ref[g], preferred_element_type=jnp.float32)
            dq_ref[:, g * width : (g + 1) * width] += lax.dot_general(
                ds, key, TN, preferred_element_type=jnp.float32
            )
        for i, start in enumerate(starts):
            rows_here = slice(i * half_rows, (i + 1) * half_rows)
            at = pl.ds(start, half_rows)
            dkv_ref[at, 0:width] = (dk[rows_here] * scale).astype(jnp.bfloat16)
            dkv_ref[at, width:] = dv[rows_here].astype(jnp.bfloat16)

    keys_values.far()
    query_heads(wqb_ref, (2, 3))
    keys_values.cross((0, -1))
    both_halves(forward, 0)
    keys_values.cross((1, 2))
    two_offsets(forward, -1)
    keys_values.finish()
    both_halves(forward, 2)

    for g in range(QUERY_PER_KEY):
        columns = slice(g * width, (g + 1) * width)
        inverse = 1.0 / jnp.sum(den_ref[g].T, axis=1, keepdims=True)
        context = (num_ref[g] * inverse).astype(jnp.bfloat16)
        context_ref[:, columns] = context
        up = (up_ref[:, columns].astype(jnp.float32) * inverse).astype(jnp.bfloat16)
        up4_ref[g] = up
        up4t_ref[g] = up.T
        product = up.astype(jnp.float32) * context.astype(jnp.float32)
        corr_ref[g] = jnp.sum(product.T, axis=0, keepdims=True)

    dkv = Scatter(torus, dkv_ref, *boxes[0:4])
    dwq = Scatter(torus, gq_ref, *boxes[4:8])
    dwkv = Scatter(torus, gkv_ref, *boxes[8:12])
    both_halves(backward, 2)
    dkv.start()
    two_offsets(backward, 1)
    dkv.turn()
    both_halves(backward, 0)
    dkv.land()

    query_gain_grads = jnp.zeros((1, width), jnp.float32)
    for g in range(QUERY_PER_KEY):
        columns = slice(g * width, (g + 1) * width)
        raw_grads, gain_grads = head_map_back(
            raw_ref[:, columns], query_gain_ref[...], cosine, sine, dq_ref[:, columns] * scale
        )
        jq_ref[:, columns] = raw_grads.astype(jnp.bfloat16)
        query_gain_grads = query_gain_grads + gain_grads

    def weight_grads(j_ref, g_ref):
        def piece(half, offset):
            starts = pieces(half, offset)
            rows = jnp.concatenate(
                [normed_ref[:, pl.ds(start, half_rows)] for start in starts], axis=1
            )
            grads = lax.dot_general(rows, j_ref[...], TN, preferred_element_type=jnp.float32)
            for i, start in enumerate(starts):
                g_ref[pl.ds(start, half_rows), :] = grads[
                    i * half_rows : (i + 1) * half_rows
                ].astype(jnp.bfloat16)

        return piece

    query_weights = weight_grads(jq_ref, gq_ref)
    both_halves(query_weights, 2)
    dwq.start()
    dkv.turn_two()
    for offset in (1, -1, 0):
        both_halves(query_weights, offset)

    def query_terms(i, carry):
        at = pl.ds(pl.multiple_of(i * 256, 256), 256)
        terms_ref[:, at] = (
            lax.dot_general(
                jq_ref[:, 0:pair_width], wqa_ref[at, :], NT, preferred_element_type=jnp.float32
            )
            + lax.dot_general(
                jq_ref[:, pair_width:], wqb_ref[at, :], NT, preferred_element_type=jnp.float32
            )
        ).astype(jnp.bfloat16)
        return carry

    lax.fori_loop(0, terms_ref.shape[1] // 256, query_terms, 0)

    def keep_dkv(at, total):
        dkv_sum_ref[at, :] = total

    dkv.finish(keep_dkv)
    raw_grads, key_gain_grads = head_map_back(
        raw_ref[:, split:], key_gain_ref[...], cosine, sine, dkv_sum_ref[:, :width]
    )
    jkv_ref[:, :width] = raw_grads.astype(jnp.bfloat16)
    jkv_ref[:, width:] = dkv_sum_ref[:, width:].astype(jnp.bfloat16)
    pair_weights = weight_grads(jkv_ref, gkv_ref)
    both_halves(pair_weights, 2)
    dwkv.start()

    def value_terms(i, carry):
        at = pl.ds(pl.multiple_of(i * 256, 256), 256)
        terms_ref[:, at] = (
            terms_ref[:, at].astype(jnp.float32)
            + lax.dot_general(jkv_ref[...], wkv_ref[at, :], NT, preferred_element_type=jnp.float32)
        ).astype(jnp.bfloat16)
        return carry

    def term_rows(step, part=None, flip=False):
        core = torus.place["core"]
        index = wrap(torus.place["z"] + step) * 2 + (1 - core if flip else core)
        size = count if part is None else count // 2
        start = index * count + (0 if part is None else part * (count // 2))
        return terms_ref.at[pl.ds(pl.multiple_of(start, count // 2), size), :]

    dwq.turn((2, 1))
    lax.fori_loop(0, terms_ref.shape[1] // 256, value_terms, 0)
    pair = {
        step: torus.send(term_rows(step, flip=True), pair_ref.at[step % SIDE], "core", 1)
        for step in (2, 1, -1, 0)
    }
    dwq.turn((-1, 0))
    for offset in (1, -1, 0):
        both_halves(pair_weights, offset)
    torus.arrive(pair[2], pair_ref.at[2])
    add_to(term_rows(2), pair_ref.at[2])
    far = {}
    for step in (1, -1):
        far[step] = torus.send(
            term_rows(2, part_of(step)), zfar_ref.at[part_of(step)], "z", step
        )
    dwkv.turn()
    for step in (1, -1):
        torus.arrive(pair[step], pair_ref.at[step % SIDE])
        add_to(term_rows(step), pair_ref.at[step % SIDE])
    dwq.land((2,))
    near = {}
    for step in (1, -1):
        torus.arrive(far[step], zfar_ref.at[part_of(step)])
        add_to(term_rows(step, part_of(step)), zfar_ref.at[part_of(step)])
        near[step] = torus.send(term_rows(step), znear_ref.at[part_of(step)], "z", step)
    dwq.land((1, -1))
    dwq.turn_two()
    torus.arrive(pair[0], pair_ref.at[0])
    for step in (1, -1):
        torus.arrive(near[step], znear_ref.at[part_of(step)])
    normed_grads = term_rows(0)[...].astype(jnp.float32) + pair_ref[0].astype(jnp.float32)
    normed_grads = normed_grads + (
        znear_ref[0].astype(jnp.float32) + znear_ref[1].astype(jnp.float32)
    )
    tokens = tokens_ref[...].astype(jnp.float32)
    inverse = inverse_rms(tokens)
    unit = tokens * inverse
    norm_gain_grads = jnp.sum(normed_grads * unit, axis=0, keepdims=True)
    scaled = normed_grads * norm_gain_ref[...]
    token_grads_ref[...] = inverse * (
        scaled - unit * jnp.mean(scaled * unit, axis=-1, keepdims=True)
    )
    lines = tokens.shape[1] // width
    gains_ref[...] = jnp.zeros_like(gains_ref)
    for i in range(lines):
        gains_ref[i : i + 1, :] = norm_gain_grads[:, i * width : (i + 1) * width]
    gains_ref[lines : lines + 1, :] = query_gain_grads
    gains_ref[lines + 1 : lines + 2, :] = key_gain_grads

    def share(axis, box):
        place, size = torus.place[axis], box.shape[0]
        box[place] = gains_ref[...]
        return [
            torus.send(box.at[place], box.at[place], axis, step) for step in range(1, size)
        ]

    def collect(axis, box, sent):
        place, size = torus.place[axis], box.shape[0]
        for step in range(1, size):
            torus.arrive(sent[step - 1], box.at[lax.rem(place + size - step, size)])
        total = box[0]
        for i in range(1, size):
            total = total + box[i]
        gains_ref[...] = total

    def keep_q(at, total):
        projection_grads_ref[at, :split] = total

    def keep_kv(at, total):
        projection_grads_ref[at, split:] = total

    sent = share("z", gz_ref)
    dwq.land((0,))
    dwkv.land((2,))
    collect("z", gz_ref, sent)
    sent = share("core", gc_ref)
    dwkv.land((1, -1))
    collect("core", gc_ref, sent)
    sent = share("x", gx_ref)
    dwkv.turn_two()
    collect("x", gx_ref, sent)
    sent = share("y", gy_ref)
    dwq.finish(keep_q)
    dwkv.land((0,))
    dwkv.finish(keep_kv)
    collect("y", gy_ref, sent)
    torus.close()


def layer(tokens, shard, norm_gain, query_gain, key_gain, segments, waves, upstream):
    rows, columns = shard.shape
    count, depth = tokens.shape
    local = upstream.shape[0]
    total = local * SIDE * SIDE
    group, width = QUERY_PER_KEY, HEAD_WIDTH
    split = group * width
    gains = (depth // width + 8, width)
    copies = 7 * 40 + 8 + 8 + 10
    bf16, f32 = jnp.bfloat16, jnp.float32
    vmem = pl.BlockSpec(memory_space=pltpu.VMEM)
    hbm = pl.BlockSpec(memory_space=pltpu.HBM)
    return pl.pallas_call(
        layer_kernel,
        out_shape=(
            jax.ShapeDtypeStruct((local, split), bf16),
            jax.ShapeDtypeStruct((count, depth), f32),
            jax.ShapeDtypeStruct((rows, columns), f32),
            jax.ShapeDtypeStruct(gains, f32),
        ),
        in_specs=[hbm] * 8,
        out_specs=(vmem,) * 4,
        scratch_shapes=[
            pltpu.SemaphoreType.DMA((copies,)),
            pltpu.SemaphoreType.DMA((copies,)),
            pltpu.SemaphoreType.DMA((10,)),
            pltpu.VMEM(tokens.shape, bf16),
            pltpu.VMEM(norm_gain.shape, f32),
            pltpu.VMEM(query_gain.shape, f32),
            pltpu.VMEM(key_gain.shape, f32),
            pltpu.VMEM(segments.shape, jnp.int32),
            pltpu.VMEM(waves.shape, f32),
            pltpu.VMEM(upstream.shape, bf16),
            pltpu.VMEM((total, 2 * width), bf16),
            pltpu.VMEM((local, split + width), f32),
            pltpu.VMEM((local, depth), bf16),
            pltpu.VMEM((depth, 2 * width), bf16),
            pltpu.VMEM((depth, split // 2), bf16),
            pltpu.VMEM((depth, split // 2), bf16),
            pltpu.VMEM((2, local, width), f32),
            pltpu.VMEM((2, local), f32),
            pltpu.VMEM((2 * SIDE, group, total // (2 * SIDE), local), bf16),
            pltpu.VMEM((group, local, width), bf16),
            pltpu.VMEM((group, width, local), bf16),
            pltpu.VMEM((group, local, width), bf16),
            pltpu.VMEM((group, width, local), bf16),
            pltpu.VMEM((group, local, width), f32),
            pltpu.VMEM((group, 8, local), f32),
            pltpu.VMEM((group, 1, local), f32),
            pltpu.VMEM((local, split), f32),
            pltpu.VMEM((total, 2 * width), bf16),
            pltpu.VMEM((local, split), bf16),
            pltpu.VMEM((local, 2 * width), bf16),
            pltpu.VMEM((depth, split), bf16),
            pltpu.VMEM((depth, 2 * width), bf16),
            pltpu.VMEM((local, 2 * width), f32),
            pltpu.VMEM((local, depth), bf16),
            pltpu.VMEM((SIDE, count, depth), bf16),
            pltpu.VMEM((2, count // 2, depth), bf16),
            pltpu.VMEM((2, count, depth), bf16),
            pltpu.VMEM((SIDE,) + gains, f32),
            pltpu.VMEM((SIDE,) + gains, f32),
            pltpu.VMEM((SIDE,) + gains, f32),
            pltpu.VMEM((2,) + gains, f32),
        ]
        + scatter_scratch(local, 2 * width)
        + scatter_scratch(rows, split)
        + scatter_scratch(rows, 2 * width),
        compiler_params=pltpu.CompilerParams(
            collective_id=0, has_side_effects=True, vmem_limit_bytes=60 * 1024 * 1024
        ),
        cost_estimate=pl.CostEstimate(
            flops=6 * local * depth * columns + 14 * group * local * total * width,
            bytes_accessed=8 * depth * columns,
            transcendentals=group * local * total,
        ),
    )(tokens, shard, norm_gain, query_gain, key_gain, segments, waves, upstream)


def finish_kernel(
    context_ref, token_ref, projection_ref, gains_ref,
    context_out, token_out, projection_out, norm_out, query_out, key_out,
    context_box, token_box, projection_box, gains_box, sems,
):
    loads, stores = [], []
    for i, (source, box, target) in enumerate(
        (
            (gains_ref, gains_box, None),
            (projection_ref, projection_box, projection_out),
            (token_ref, token_box, token_out),
            (context_ref, context_box, context_out),
        )
    ):
        loads.append(pltpu.make_async_copy(source, box, sems.at[2 * i]))
        if target is not None:
            stores.append(pltpu.make_async_copy(box, target, sems.at[2 * i + 1]))
        loads[-1].start()
    loads[0].wait()
    lines = norm_out.shape[0]
    norm_out[...] = gains_box[0:lines, :]
    query_out[...] = gains_box[lines : lines + 1, :]
    key_out[...] = gains_box[lines + 1 : lines + 2, :]
    for load, store in zip(loads[1:], stores):
        load.wait()
        store.start()
    for store in stores:
        store.wait()


def finish(context, token_grads, projection_grads, gains):
    width = HEAD_WIDTH
    vmem = pl.BlockSpec(memory_space=pltpu.VMEM)
    hbm = pl.BlockSpec(memory_space=pltpu.HBM)
    f32 = jnp.float32
    arrays = (context, token_grads, projection_grads)
    return pl.pallas_call(
        finish_kernel,
        out_shape=tuple(jax.ShapeDtypeStruct(array.shape, array.dtype) for array in arrays)
        + (
            jax.ShapeDtypeStruct((token_grads.shape[1] // width, width), f32),
            jax.ShapeDtypeStruct((1, width), f32),
            jax.ShapeDtypeStruct((1, width), f32),
        ),
        in_specs=[hbm] * 4,
        out_specs=(hbm,) * 3 + (vmem,) * 3,
        scratch_shapes=[pltpu.VMEM(array.shape, array.dtype) for array in arrays + (gains,)]
        + [pltpu.SemaphoreType.DMA((8,))],
        compiler_params=pltpu.CompilerParams(vmem_limit_bytes=60 * 1024 * 1024),
    )(*arrays, gains)


def rope_waves(local, blocks, width):
    half = width // 2
    frequency = THETA ** (-2.0 * np.arange(half) / width)
    frequency = np.concatenate([frequency, frequency])
    sign = np.concatenate([-np.ones(half), np.ones(half)])
    near = np.arange(local)[:, None] * frequency[None, :]
    far = np.arange(blocks)[:, None] * float(local) * frequency[None, :]
    waves = [np.cos(near), np.sin(near), np.cos(far), np.sin(far), sign * np.cos(far), sign * np.sin(far)]
    return np.concatenate(waves, axis=0).astype(np.float32)


def on_device(tokens, projection, norm_gain, query_gain, key_gain, segment_ids, context_cotangent):
    local = context_cotangent.shape[0]
    waves = jnp.asarray(rope_waves(local, SIDE * SIDE, HEAD_WIDTH))
    norm_gain = norm_gain.reshape(1, -1)
    query_gain = query_gain.reshape(1, -1)
    key_gain = key_gain.reshape(1, -1)
    segments = segment_ids.reshape(-1, 128)
    context, token_grads, projection_grads, gains = layer(
        tokens, projection, norm_gain, query_gain, key_gain, segments, waves, context_cotangent
    )
    context, token_grads, projection_grads, norm_gains, query_gains, key_gains = finish(
        context, token_grads, projection_grads, gains
    )
    return (
        context,
        token_grads,
        projection_grads,
        norm_gains.reshape(-1),
        query_gains.reshape(-1),
        key_gains.reshape(-1),
    )


def solution(mesh):
    placed = (
        P(("dp", "ctx", "tp"), None),
        P("ctx", "tp"),
        P(),
        P(),
        P(),
        P("dp"),
        P(("dp", "ctx"), "tp"),
    )
    return jax.shard_map(
        on_device,
        mesh=mesh,
        in_specs=placed,
        out_specs=(
            P(("dp", "ctx"), "tp"),
            P(("dp", "ctx", "tp"), None),
            P(("dp", "ctx"), "tp"),
            P("dp"),
            P("dp"),
            P("dp"),
        ),
        check_vma=False,
    )
```
